512 devices in a mesh: line: 16 (over z), py: 8 (over y, core), pz: 4 (over x).
Axes of the slice: x: 4, y: 4, z: 16, core: 2. Of those that a mesh axis runs over, the one named last changes fastest.
Arguments:
- fluxes: float32 [3, 128, 5, 32, 512], P(None, 'line', None, 'py', 'pz'), may hold values from -6 to 6
- jacobian: float32 [128, 5, 5, 32, 512], P('line', None, None, 'py', 'pz'), may hold values from -48 to 48, as said below
- dissipation: float32 [128, 32, 512], P('line', 'py', 'pz'), may hold values from 0.1 to 2
Outputs:
- update: float32 [128, 5, 32, 512], P('line', None, 'py', 'pz')
The draws below stay inside these ranges and needn't reach their ends.
Inputs may be any that keep to these rules, and one draw needn't show every extreme that they name: jacobian[i, a, b, j, k] equals jacobian[i, b, a, j, k].
All inputs are finite; a program needn't handle non-finite values.
Results may differ from the reference program's by a relative error of at most 0.0003.
Values sent between devices are 32-bit elements; how exact they have to be, the bound alone decides.
A program may use at most 64 MiB of HBM per device.

```python
import math
import jax
import jax.numpy as jnp
from jax import lax

NX = 128
NY = 32
NZ = 512


def draw_jacobian(key, part):
    key_entries = jax.random.fold_in(key, 11)
    key_scales = jax.random.fold_in(key, 12)
    full_shape = (NX, 5, 5, NY, NZ)
    scale_shape = (NX, 1, 1, NY, NZ)
    entries = jax.random.truncated_normal(key_entries, -4.0, 4.0, full_shape, jnp.float32)
    scales = jnp.exp(jax.random.uniform(key_scales, scale_shape, jnp.float32, math.log(2.0), math.log(12.0)))
    return 0.5 * (entries + jnp.swapaxes(entries, 1, 2)) * scales


def block_scale(key, shape, pieces, low, top_value):
    factor_of = 1.0
    for dim, shards_of in pieces:
        steps = jax.random.uniform(jax.random.fold_in(jax.random.fold_in(key, 6), dim), (shards_of,), jnp.float32, low / len(pieces), top_value / len(pieces))
        factor_of = factor_of * jnp.repeat(jnp.exp(steps), shape[dim] // shards_of).reshape((-1,) + (1,) * (len(shape) - 1 - dim))
    return factor_of


def scatter_about(stream_key, dims, deviation, bound, split=(), kind=jnp.bfloat16):
    values = jax.random.normal(stream_key, dims, jnp.float32) * deviation
    if len(split) > 0:
        values = block_scale(stream_key, dims, split, -0.22, 0.18) * values
    return jnp.clip(values, min=-bound, max=bound).astype(kind)


def setup_inputs(seed: int = 0) -> dict:
    key_of = jax.random.split(jax.random.key(seed), 4)
    fluxes = scatter_about(key_of[0], (3, NX, 5, NY, NZ), 1.0, 6.0, ((1, 16), (3, 8), (4, 4)), jnp.float32)
    jacobian = draw_jacobian(jax.random.fold_in(key_of[3], 71), 0)
    dissipation = jnp.clip(jnp.exp(math.log(2.0) - 2.9957323 * jax.random.uniform(key_of[2], (NX, NY, NZ), jnp.float32) ** block_scale(key_of[2], (NX, NY, NZ), ((0, 16), (1, 8), (2, 4)), -0.2, 0.2)), 0.1, 2.0)
    return {"fluxes": fluxes, "jacobian": jacobian, "dissipation": dissipation}


def mat_mul(left_mat, right_mat):
    extent = left_mat.shape[-2]
    total = left_mat[..., :, 0:1, :] * right_mat[..., 0:1, :, :]
    for index in range(1, extent):
        total = total + left_mat[..., :, index:index + 1, :] * right_mat[..., index:index + 1, :, :]
    return total


def solve_small(matrix, sides):
    extent = matrix.shape[0]
    mat_rows = [matrix[index] for index in range(extent)]
    side_rows = [sides[index] for index in range(extent)]
    for column in range(extent):
        scaling = 1.0 / mat_rows[column][column]
        mat_rows[column] = mat_rows[column] * scaling[None]
        side_rows[column] = side_rows[column] * scaling[None]
        for target in range(extent):
            if target != column:
                factor = mat_rows[target][column]
                mat_rows[target] = mat_rows[target] - factor[None] * mat_rows[column]
                side_rows[target] = side_rows[target] - factor[None] * side_rows[column]
    return jnp.stack(side_rows)


def block_thomas(lower, diagonal, upper, right):
    def forward(carried, row):
        prev_upper, prev_right = carried
        lower_row, diag_row, upper_row, right_row = row
        pivot_mat = diag_row - mat_mul(lower_row, prev_upper)
        columns = upper_row.shape[1]
        joined = jnp.concatenate([upper_row, right_row - mat_mul(lower_row, prev_right)], axis=1)
        solved = solve_small(pivot_mat, joined)
        result = (solved[:, :columns], solved[:, columns:])
        return result, result

    start_state = (jnp.zeros_like(upper[0]), jnp.zeros_like(right[0]))
    _, (uppers, rights) = lax.scan(forward, start_state, (lower, diagonal, upper, right))

    def backward(later, row):
        upper_row, right_row = row
        result = right_row - mat_mul(upper_row, later)
        return result, result

    final_row = rights[-1]
    _, earlier = lax.scan(backward, final_row, (uppers[:-1], rights[:-1]), reverse=True)
    return jnp.concatenate([earlier, final_row[None]], axis=0)


def solve_plane(planes):
    jac_plane, diss_plane, right_plane = planes
    zero_face = jnp.zeros_like(jac_plane[:1])
    lower = -jnp.concatenate([zero_face, jac_plane[:-1]], axis=0)
    upper = jnp.concatenate([jac_plane[:-1], zero_face], axis=0)
    identity = jnp.eye(5, dtype=diss_plane.dtype)
    diagonal = identity[None, :, :, None] * (1.0 + diss_plane)[:, None, None, :]
    return block_thomas(lower, diagonal, upper, right_plane[:, :, None, :])[:, :, 0, :]


def reference(fluxes, jacobian, dissipation):
    flux_x = jnp.pad(fluxes[0], ((1, 1), (0, 0), (0, 0), (0, 0)))
    flux_y = jnp.pad(fluxes[1], ((0, 0), (0, 0), (1, 1), (0, 0)))
    flux_z = jnp.pad(fluxes[2], ((0, 0), (0, 0), (0, 0), (1, 1)))
    right = -0.5 * ((flux_x[2:] - flux_x[:-2]) + (flux_y[:, :, 2:] - flux_y[:, :, :-2]) + (flux_z[..., 2:] - flux_z[..., :-2]))
    jac_moved = jnp.moveaxis(jacobian, 3, 0)
    diss_moved = jnp.moveaxis(dissipation, 1, 0)
    right_moved = jnp.moveaxis(right, 2, 0)
    solved = lax.map(solve_plane, (jac_moved, diss_moved, right_moved))
    return jnp.moveaxis(solved, 0, 2)
```

```python
import functools

import jax
import jax.numpy as jnp
from jax import lax
from jax.experimental import pallas as pl
from jax.experimental.pallas import tpu as pltpu
from jax.sharding import PartitionSpec as P

MESH = pl.DeviceIdType.MESH
B = 5
SYM = [(i, j) for i in range(B) for j in range(i, B)]
POS = {}
for _n, (_i, _j) in enumerate(SYM):
    POS[_i, _j] = POS[_j, _i] = _n
NSYM = len(SYM)
GL, GR, CC = 0, NSYM, 2 * NSYM
NMAT = 2 * NSYM + B * B
MROWS = 56
GROWS = 16


def total(terms):
    result = terms[0]
    for term in terms[1:]:
        result = result + term
    return result


def sym_inverse(a):
    a = list(a)
    for k in range(B):
        scaling = 1.0 / a[POS[k, k]]
        col = {i: a[POS[i, k]] for i in range(B) if i != k}
        scaled = {i: col[i] * scaling for i in col}
        for i, j in SYM:
            if i != k and j != k:
                a[POS[i, j]] = a[POS[i, j]] - scaled[i] * col[j]
        for i in col:
            a[POS[i, k]] = scaled[i]
        a[POS[k, k]] = -scaling
    return [-entry for entry in a]


def sym_times(inv, mat):
    return [[total([inv[POS[i, k]] * mat[k][j] for k in range(B)]) for j in range(B)] for i in range(B)]


def mat_vec(mat, vec):
    return [total([mat[i][k] * vec[k] for k in range(B)]) for i in range(B)]


def sym_vec(mat, vec):
    return [total([mat[POS[i, k]] * vec[k] for k in range(B)]) for i in range(B)]


def transposed(mat):
    return [[mat[j][i] for j in range(B)] for i in range(B)]


def product_sym(left, right):
    return [total([left[i][k] * right[k][j] for k in range(B)]) for i, j in SYM]


def product(left, right):
    return [[total([left[i][k] * right[k][j] for k in range(B)]) for j in range(B)] for i in range(B)]


def as_mat(flat):
    return [[flat[i * B + j] for j in range(B)] for i in range(B)]


def kernel(
    n,
    npy,
    npz,
    flux_hbm,
    jac_hbm,
    diss_hbm,
    out_ref,
    fv,
    jv,
    dv,
    xl,
    xr,
    yl,
    yr,
    zl,
    zr,
    ysl,
    ysr,
    zsl,
    zsr,
    rv,
    el,
    facs,
    gel,
    yv,
    msend,
    mrecv,
    gsend,
    grecv,
    sfac,
    sol,
    xrecv,
    lsem,
    hsend,
    hrecv,
    m_s,
    m_r,
    g_s,
    g_r,
    x_s,
    x_r,
):
    p = lax.axis_index("line")
    py = lax.axis_index("py")
    pz = lax.axis_index("pz")
    core = lax.rem(py, 2)
    ncell = jv.shape[0] // (B * B)
    solver = [4 * s + 2 * core for s in range(4)]
    is_solver = lax.rem(p + n - 2 * core, 4) == 0
    mine = lax.div(p, 4)

    barrier = pltpu.get_barrier_semaphore()
    peers = [{"line": lax.rem(p + o, n)} for o in range(1, n)]
    peers += [{"py": lax.rem(py + o, npy)} for o in (1, npy - 1)]
    peers += [{"pz": lax.rem(pz + o, npz)} for o in (1, npz - 1)]
    for peer in peers:
        pl.semaphore_signal(barrier, inc=1, device_id=peer, device_id_type=MESH)

    loads = [
        pltpu.make_async_copy(flux_hbm, fv, lsem.at[0]),
        pltpu.make_async_copy(jac_hbm, jv, lsem.at[1]),
        pltpu.make_async_copy(diss_hbm, dv, lsem.at[2]),
    ]
    for load in loads:
        load.start()
    sol[...] = jnp.zeros_like(sol)
    msend[...] = jnp.zeros_like(msend)
    gsend[...] = jnp.zeros_like(gsend)
    ncomp = ncell * B
    shape = (4, 128)
    row = lax.broadcasted_iota(jnp.int32, shape, 0)
    lane = lax.broadcasted_iota(jnp.int32, shape, 1)
    zero = jnp.zeros(shape, jnp.float32)
    loads[0].wait()

    packed_l, packed_r = zero, zero
    for k in range(ncomp):
        cell = k // B
        f_after = fv[0, k + B] if cell < ncell - 1 else zero
        f_before = fv[0, k - B] if cell > 0 else zero
        g = fv[1, k]
        h = fv[2, k]
        blank = jnp.zeros((1, 128), jnp.float32)
        dy = jnp.concatenate([g[1:], blank], 0) - jnp.concatenate([blank, g[:-1]], 0)
        h_after = jnp.where(lane == 127, 0.0, pltpu.roll(h, 127, 1))
        h_before = jnp.where(lane == 0, 0.0, pltpu.roll(h, 1, 1))
        rv[k] = -0.5 * ((f_after - f_before) + dy + (h_after - h_before))
        ysl[k : k + 1, :] = g[0:1]
        ysr[k : k + 1, :] = g[3:4]
        packed_l = jnp.where(lane == k, pltpu.roll(h, k, 1), packed_l)
        packed_r = jnp.where(lane == k, pltpu.roll(h, (k + 1) % 128, 1), packed_r)
    zsl[...] = packed_l
    zsr[...] = packed_r

    loads[1].wait()
    loads[2].wait()

    def first_level(j, carry):
        m = 2 * j + 1
        cut = jnp.logical_and(m == ncell - 1, p == n - 1)
        keep = jnp.where(cut, 0.0, 1.0)
        before = [jv[(m - 1) * B * B + i * B + k] for i, k in SYM]
        after = [jv[m * B * B + i * B + k] * keep for i, k in SYM]
        inv = 1.0 / (1.0 + dv[m])
        full_b = [[before[POS[i, k]] for k in range(B)] for i in range(B)]
        full_a = [[after[POS[i, k]] for k in range(B)] for i in range(B)]
        scaled_b = [[(before[POS[i, k]] * inv) for k in range(B)] for i in range(B)]
        scaled_a = [[(after[POS[i, k]] * inv) for k in range(B)] for i in range(B)]
        for e, value in enumerate(product_sym(full_b, scaled_b)):
            el[j * NMAT + GL + e] = value
        for e, value in enumerate(product_sym(full_a, scaled_a)):
            el[j * NMAT + GR + e] = value
        couple = product(full_a, scaled_b)
        for e in range(B * B):
            el[j * NMAT + CC + e] = couple[e // B][e % B]
        return carry

    lax.fori_loop(0, ncell // 2, first_level, 0)

    def merge(i, carry):
        a, b, new = 2 * i * NMAT, (2 * i + 1) * NMAT, (4 + i) * NMAT
        m = jnp.where(i == 2, 4, 2 + 4 * i)
        pivot = [el[a + GR + e] + el[b + GL + e] for e in range(NSYM)]
        diag = 1.0 + dv[m]
        for k in range(B):
            pivot[POS[k, k]] = pivot[POS[k, k]] + diag
        inv = sym_inverse(pivot)
        ca = as_mat([el[a + CC + e] for e in range(B * B)])
        cb = as_mat([el[b + CC + e] for e in range(B * B)])
        w = sym_times(inv, ca)
        u = sym_times(inv, transposed(cb))
        gl_new = product_sym(transposed(ca), w)
        gr_new = product_sym(cb, u)
        c_new = product(cb, w)
        for e in range(NSYM):
            el[new + GL + e] = el[a + GL + e] - gl_new[e]
            el[new + GR + e] = el[b + GR + e] - gr_new[e]
            facs[i * 65 + e] = inv[e]
        for e in range(B * B):
            el[new + CC + e] = c_new[e // B][e % B]
            facs[i * 65 + NSYM + e] = w[e // B][e % B]
            facs[i * 65 + NSYM + B * B + e] = u[e // B][e % B]
        return carry

    lax.fori_loop(0, 3, merge, 0)

    diag0 = 1.0 + dv[0]
    for e in range(NMAT):
        value = el[6 * NMAT + e]
        if e < NSYM and SYM[e][0] == SYM[e][1]:
            value = value + diag0
        msend[pl.ds(e, 4, stride=MROWS), :] = value

    pl.semaphore_wait(barrier, len(peers))

    halo = []

    def send_halo(src, dst, index, peer):
        copy = pltpu.make_async_remote_copy(
            src_ref=src,
            dst_ref=dst,
            send_sem=hsend.at[index],
            recv_sem=hrecv.at[index],
            device_id=peer,
            device_id_type=MESH,
        )
        copy.start()
        halo.append(copy)

    send_halo(fv.at[0, pl.ds(ncomp - B, B)], xl, 0, {"line": lax.rem(p + 1, n)})
    send_halo(fv.at[0, pl.ds(0, B)], xr, 1, {"line": lax.rem(p + n - 1, n)})
    send_halo(ysr, yl, 2, {"py": lax.rem(py + 1, npy)})
    send_halo(ysl, yr, 3, {"py": lax.rem(py + npy - 1, npy)})
    send_halo(zsr, zl, 4, {"pz": lax.rem(pz + 1, npz)})
    send_halo(zsl, zr, 5, {"pz": lax.rem(pz + npz - 1, npz)})

    def part_copies(src, dst, rows, send_sem, recv_sem, s):
        here = src.at[pl.ds(s * rows, rows)]
        there = dst.at[pl.ds(pl.multiple_of(p * rows, 8), rows)]
        away = pltpu.make_async_remote_copy(
            src_ref=here,
            dst_ref=there,
            send_sem=send_sem.at[s],
            recv_sem=recv_sem.at[p],
            device_id={"line": solver[s]},
            device_id_type=MESH,
        )
        return away, pltpu.make_async_copy(here, there, send_sem.at[s])

    def start_parts(src, dst, rows, send_sem, recv_sem):
        for s in range(4):
            away, near = part_copies(src, dst, rows, send_sem, recv_sem, s)
            pl.when(solver[s] != p)(away.start)
            pl.when(solver[s] == p)(near.start)

    def finish_parts(src, dst, rows, send_sem, recv_sem):
        for s in range(4):
            away, near = part_copies(src, dst, rows, send_sem, recv_sem, s)
            pl.when(solver[s] != p)(away.wait_send)
            pl.when(solver[s] == p)(near.wait)

    def await_parts(src, dst, rows, send_sem, recv_sem):
        def one(q, carry):
            copy = pltpu.make_async_remote_copy(
                src_ref=src.at[pl.ds(0, rows)],
                dst_ref=dst.at[pl.ds(pl.multiple_of(q * rows, 8), rows)],
                send_sem=send_sem.at[0],
                recv_sem=recv_sem.at[q],
                device_id={"line": solver[0]},
                device_id_type=MESH,
            )
            pl.when(q != p)(copy.wait_recv)
            return carry

        lax.fori_loop(0, n, one, 0)

    mats = (msend, mrecv, MROWS, m_s, m_r)
    sides = (gsend, grecv, GROWS, g_s, g_r)
    start_parts(*mats)

    for copy in halo:
        copy.wait_recv()

    x_first = jnp.where(p > 0, 0.5, 0.0)
    x_last = jnp.where(p < n - 1, -0.5, 0.0)
    y_first = jnp.where(row == 0, jnp.where(py > 0, 0.5, 0.0), 0.0)
    y_last = jnp.where(row == 3, jnp.where(py < npy - 1, -0.5, 0.0), 0.0)
    z_first = jnp.where(lane == 0, jnp.where(pz > 0, 0.5, 0.0), 0.0)
    z_last = jnp.where(lane == 127, jnp.where(pz < npz - 1, -0.5, 0.0), 0.0)
    z_left, z_right = zl[...], zr[...]
    for k in range(ncomp):
        value = rv[k] + y_first * yl[k : k + 1, :] + y_last * yr[k : k + 1, :]
        value = value + z_first * pltpu.roll(z_left, (128 - k) % 128, 1)
        value = value + z_last * pltpu.roll(z_right, 127 - k, 1)
        if k < B:
            value = value + x_first * xl[k]
        if k >= ncomp - B:
            value = value + x_last * xr[k - ncomp + B]
        rv[k] = value

    def sym_face(f):
        return [jv[f * B * B + i * B + k] for i, k in SYM]

    keep_last = jnp.where(p == n - 1, 0.0, 1.0)
    g_left, g_right = [None] * 7, [None] * 7
    for j in range(ncell // 2):
        m = 2 * j + 1
        inv = 1.0 / (1.0 + dv[m])
        scaled = [rv[m * B + i] * inv for i in range(B)]
        g_left[j] = [-v for v in sym_vec(sym_face(m - 1), scaled)]
        after = scaled if m < ncell - 1 else [v * keep_last for v in scaled]
        g_right[j] = sym_vec(sym_face(m), after)
    for i, m in enumerate((2, 6, 4)):
        a, b = 2 * i, 2 * i + 1
        q = [rv[m * B + c] + g_right[a][c] + g_left[b][c] for c in range(B)]
        w = as_mat([facs[i * 65 + NSYM + e] for e in range(B * B)])
        u = as_mat([facs[i * 65 + NSYM + B * B + e] for e in range(B * B)])
        more_l = mat_vec(transposed(w), q)
        more_r = mat_vec(transposed(u), q)
        g_left[4 + i] = [g_left[a][c] + more_l[c] for c in range(B)]
        g_right[4 + i] = [g_right[b][c] + more_r[c] for c in range(B)]
        for c in range(B):
            gel[i * B + c] = q[c]
    for c in range(B):
        gsend[pl.ds(c, 4, stride=GROWS), :] = rv[c] + g_left[6][c]
        gsend[pl.ds(B + c, 4, stride=GROWS), :] = g_right[6][c]

    start_parts(*sides)
    for i in range(3):
        value = sym_vec([facs[i * 65 + e] for e in range(NSYM)], [gel[i * B + c] for c in range(B)])
        for c in range(B):
            yv[i * B + c] = value[c]

    def answer_copy(q):
        return pltpu.make_async_remote_copy(
            src_ref=sol.at[pl.ds(pl.multiple_of(q * 8, 8), 16)],
            dst_ref=xrecv.at[pl.ds(pl.multiple_of(mine * 16, 16), 16)],
            send_sem=x_s.at[q],
            recv_sem=x_r.at[mine],
            device_id={"line": q},
            device_id_type=MESH,
        )

    own_answer = pltpu.make_async_copy(
        sol.at[pl.ds(pl.multiple_of(p * 8, 8), 16)],
        xrecv.at[pl.ds(pl.multiple_of(mine * 16, 16), 16)],
        x_s.at[p],
    )

    def solve():
        finish_parts(*mats)
        await_parts(*mats)

        def even(e):
            return mrecv[pl.ds(e, 8, stride=2 * MROWS), :]

        def odd(e):
            return mrecv[pl.ds(MROWS + e, 8, stride=2 * MROWS), :]

        inv0 = sym_inverse([odd(GL + e) + even(GR + e) for e in range(NSYM)])
        ca = as_mat([even(CC + e) for e in range(B * B)])
        cb = as_mat([odd(CC + e) for e in range(B * B)])
        w0 = sym_times(inv0, ca)
        u0 = sym_times(inv0, transposed(cb))
        less_l = product_sym(transposed(ca), w0)
        less_r = product_sym(cb, u0)
        diag = [even(GL + e) - less_l[e] + pltpu.roll(odd(GR + e) - less_r[e], 1, 0) for e in range(NSYM)]
        couple = product(cb, w0)
        base = 0

        def keep(values):
            nonlocal base
            start = base
            for value in values:
                sfac[base] = value
                base += 1
            return start

        def flat(mat):
            return [entry for line in mat for entry in line]

        at_inv0, at_w0, at_u0 = keep(inv0), keep(flat(w0)), keep(flat(u0))
        levels = []
        for step in (1, 2, 4):
            inv = sym_inverse(diag)
            left = [[pltpu.roll(entry, step, 0) for entry in line] for line in couple]
            w = sym_times(inv, left)
            u = sym_times(inv, transposed(couple))
            levels.append((step, keep(flat(w)), keep(flat(u))))
            less_l = product_sym(transposed(left), w)
            less_r = product_sym(couple, u)
            diag = [
                diag[e] - pltpu.roll(less_l[e], 8 - step, 0) - pltpu.roll(less_r[e], step, 0)
                for e in range(NSYM)
            ]
            if step < 4:
                couple = [[pltpu.roll(v, 8 - step, 0) for v in line] for line in product(couple, w)]
        at_last = keep(sym_inverse(diag))

        finish_parts(*sides)
        await_parts(*sides)

        def saved(start, count):
            return [sfac[start + e] for e in range(count)]

        def even_side(e):
            return grecv[pl.ds(e, 8, stride=2 * GROWS), :]

        def odd_side(e):
            return grecv[pl.ds(GROWS + e, 8, stride=2 * GROWS), :]

        w0 = as_mat(saved(at_w0, B * B))
        u0 = as_mat(saved(at_u0, B * B))
        q = [odd_side(c) + even_side(B + c) for c in range(B)]
        more_l = mat_vec(transposed(w0), q)
        more_r = mat_vec(transposed(u0), q)
        side = [
            even_side(c) + more_l[c] + pltpu.roll(odd_side(B + c) + more_r[c], 1, 0) for c in range(B)
        ]
        for step, at_w, at_u in levels:
            more_l = mat_vec(transposed(as_mat(saved(at_w, B * B))), side)
            more_r = mat_vec(transposed(as_mat(saved(at_u, B * B))), side)
            side = [
                side[c] + pltpu.roll(more_l[c], 8 - step, 0) + pltpu.roll(more_r[c], step, 0)
                for c in range(B)
            ]
        x_even = sym_vec(saved(at_last, NSYM), side)
        x_next = [pltpu.roll(v, 7, 0) for v in x_even]
        own = sym_vec(saved(at_inv0, NSYM), q)
        from_l = mat_vec(w0, x_even)
        from_r = mat_vec(u0, x_next)
        for c in range(B):
            sol[pl.ds(c, 8, stride=16), :] = x_even[c]
            sol[pl.ds(8 + c, 8, stride=16), :] = own[c] + from_l[c] + from_r[c]

        def send_one(q, carry):
            pl.when(q != p)(answer_copy(q).start)
            return carry

        lax.fori_loop(0, n, send_one, 0)
        own_answer.start()
        own_answer.wait()

    pl.when(is_solver)(solve)

    for s in range(4):
        copy = pltpu.make_async_remote_copy(
            src_ref=sol.at[pl.ds(0, 16)],
            dst_ref=xrecv.at[pl.ds(s * 16, 16)],
            send_sem=x_s.at[0],
            recv_sem=x_r.at[s],
            device_id={"line": solver[s]},
            device_id_type=MESH,
        )
        pl.when(solver[s] != p)(copy.wait_recv)

    x = [None] * (ncell + 1)
    x[0] = [xrecv[pl.ds(c, 4, stride=16), :] for c in range(B)]
    x[ncell] = [xrecv[pl.ds(8 + c, 4, stride=16), :] for c in range(B)]
    for i, (m, a, b) in ((2, (4, 0, 8)), (0, (2, 0, 4)), (1, (6, 4, 8))):
        w = as_mat([facs[i * 65 + NSYM + e] for e in range(B * B)])
        u = as_mat([facs[i * 65 + NSYM + B * B + e] for e in range(B * B)])
        from_l, from_r = mat_vec(w, x[a]), mat_vec(u, x[b])
        x[m] = [yv[i * B + c] + from_l[c] + from_r[c] for c in range(B)]
    for m in range(1, ncell, 2):
        inv = 1.0 / (1.0 + dv[m])
        from_l = sym_vec(sym_face(m - 1), x[m - 1])
        after = x[m + 1] if m < ncell - 1 else [v * keep_last for v in x[m + 1]]
        from_r = sym_vec(sym_face(m), after)
        x[m] = [(rv[m * B + c] + from_l[c] - from_r[c]) * inv for c in range(B)]
    for m in range(ncell):
        for c in range(B):
            out_ref[m * B + c] = x[m][c]

    for copy in halo:
        copy.wait_send()

    def others():
        finish_parts(*mats)
        finish_parts(*sides)

    pl.when(jnp.logical_not(is_solver))(others)

    def answers_sent():
        def one(q, carry):
            pl.when(q != p)(answer_copy(q).wait_send)
            return carry

        lax.fori_loop(0, n, one, 0)

    pl.when(is_solver)(answers_sent)


def per_device(sizes, fluxes, jacobian, dissipation):
    n, npy, npz = sizes
    ncell = jacobian.shape[0]
    tail = jacobian.shape[3:]
    f32 = jnp.float32
    vmem, dma = pltpu.VMEM, pltpu.SemaphoreType.DMA
    tile = lambda count: vmem((count,) + tail, f32)
    flat = lambda rows: vmem((rows, 128), f32)
    ncomp = ncell * B
    out = pl.pallas_call(
        functools.partial(kernel, n, npy, npz),
        out_shape=jax.ShapeDtypeStruct((ncomp,) + tail, f32),
        in_specs=[pl.BlockSpec(memory_space=pl.ANY)] * 3,
        out_specs=pl.BlockSpec(memory_space=pltpu.VMEM),
        scratch_shapes=[
            vmem((3, ncomp) + tail, f32),
            tile(ncell * B * B),
            tile(ncell),
            tile(B),
            tile(B),
            flat(ncomp),
            flat(ncomp),
            vmem(tail, f32),
            vmem(tail, f32),
            flat(ncomp),
            flat(ncomp),
            vmem(tail, f32),
            vmem(tail, f32),
            tile(ncomp),
            tile(7 * NMAT),
            tile(3 * 65),
            tile(3 * B),
            tile(3 * B),
            flat(4 * MROWS),
            flat(n * MROWS),
            flat(4 * GROWS),
            flat(n * GROWS),
            vmem((256, 8, 128), f32),
            flat((n + 1) * 8),
            flat(4 * 16),
            dma((3,)),
            dma((6,)),
            dma((6,)),
            dma((4,)),
            dma((n,)),
            dma((4,)),
            dma((n,)),
            dma((n,)),
            dma((4,)),
        ],
        compiler_params=pltpu.CompilerParams(
            collective_id=0, has_side_effects=True, vmem_limit_bytes=32 * 1024 * 1024
        ),
    )(
        fluxes.reshape((3, ncomp) + tail),
        jacobian.reshape((ncell * B * B,) + tail),
        dissipation,
    )
    return out.reshape((ncell, B) + tail)


def solution(mesh):
    sizes = tuple(mesh.shape[name] for name in ("line", "py", "pz"))
    return jax.shard_map(
        functools.partial(per_device, sizes),
        mesh=mesh,
        in_specs=(
            P(None, "line", None, "py", "pz"),
            P("line", None, None, "py", "pz"),
            P("line", "py", "pz"),
        ),
        out_specs=P("line", None, "py", "pz"),
        check_vma=False,
    )
```

```python
import functools

import jax
import jax.numpy as jnp
from jax import lax
from jax.experimental import pallas as pl
from jax.experimental.pallas import tpu as pltpu
from jax.sharding import PartitionSpec as P

MESH = pl.DeviceIdType.MESH
B = 5
SYM = [(i, j) for i in range(B) for j in range(i, B)]
POS = {}
for _n, (_i, _j) in enumerate(SYM):
    POS[_i, _j] = POS[_j, _i] = _n
NSYM = len(SYM)
GL, GR, CC = 0, NSYM, 2 * NSYM
NMAT = 2 * NSYM + B * B
MROWS = 56
SOLVERS = ((2, 3, 4, 5), (12, 13, 14, 15))
GROWS = 16
GSEND = 2 * B


def total(terms):
    result = terms[0]
    for term in terms[1:]:
        result = result + term
    return result


def sym_inverse(a):
    a = list(a)
    for k in range(B):
        scaling = 1.0 / a[POS[k, k]]
        col = {i: a[POS[i, k]] for i in range(B) if i != k}
        scaled = {i: col[i] * scaling for i in col}
        for i, j in SYM:
            if i != k and j != k:
                a[POS[i, j]] = a[POS[i, j]] - scaled[i] * col[j]
        for i in col:
            a[POS[i, k]] = scaled[i]
        a[POS[k, k]] = -scaling
    return [-entry for entry in a]


def sym_times(inv, mat):
    return [[total([inv[POS[i, k]] * mat[k][j] for k in range(B)]) for j in range(B)] for i in range(B)]


def mat_vec(mat, vec):
    return [total([mat[i][k] * vec[k] for k in range(B)]) for i in range(B)]


def sym_vec(mat, vec):
    return [total([mat[POS[i, k]] * vec[k] for k in range(B)]) for i in range(B)]


def transposed(mat):
    return [[mat[j][i] for j in range(B)] for i in range(B)]


def product_sym(left, right):
    return [total([left[i][k] * right[k][j] for k in range(B)]) for i, j in SYM]


def product(left, right):
    return [[total([left[i][k] * right[k][j] for k in range(B)]) for j in range(B)] for i in range(B)]


def as_mat(flat):
    return [[flat[i * B + j] for j in range(B)] for i in range(B)]


def kernel(
    n,
    npy,
    npz,
    flux_hbm,
    jac_hbm,
    diss_hbm,
    out_ref,
    fv,
    jv,
    dv,
    xl,
    xr,
    yl,
    yr,
    zl,
    zr,
    ysl,
    ysr,
    zsl,
    zsr,
    rv,
    el,
    facs,
    gel,
    yv,
    msend,
    mrecv,
    gsend,
    grecv,
    sfac,
    sol,
    xrecv,
    lsem,
    hsend,
    hrecv,
    m_s,
    m_r,
    g_s,
    g_r,
    x_s,
    x_r,
):
    p = lax.axis_index("line")
    py = lax.axis_index("py")
    pz = lax.axis_index("pz")
    core = lax.rem(py, 2)
    ncell = jv.shape[0] // (B * B)
    solver = [jnp.where(core == 0, SOLVERS[0][s], SOLVERS[1][s]) for s in range(4)]
    mine = sum(jnp.where(p == solver[s], s, 0) for s in range(4))
    solvers_here = sum(jnp.where(p == solver[s], 1, 0) for s in range(4))
    is_solver = solvers_here > 0

    barrier = pltpu.get_barrier_semaphore()
    peers = [{"line": lax.rem(p + o, n)} for o in (1, n - 1)]
    peers += [{"py": lax.rem(py + o, npy)} for o in (1, npy - 1)]
    peers += [{"pz": lax.rem(pz + o, npz)} for o in (1, npz - 1)]
    for peer in peers:
        pl.semaphore_signal(barrier, inc=1, device_id=peer, device_id_type=MESH)

    def greet_line():
        def one(o, carry):
            far = {"line": lax.rem(p + o, n)}
            pl.semaphore_signal(barrier, inc=1, device_id=far, device_id_type=MESH)
            return carry

        lax.fori_loop(1, n, one, 0)

    pl.when(is_solver)(greet_line)

    loads = [
        pltpu.make_async_copy(flux_hbm, fv, lsem.at[0]),
        pltpu.make_async_copy(jac_hbm, jv, lsem.at[1]),
        pltpu.make_async_copy(diss_hbm, dv, lsem.at[2]),
    ]
    for load in loads:
        load.start()
    sol[...] = jnp.zeros_like(sol)
    msend[...] = jnp.zeros_like(msend)
    gsend[...] = jnp.zeros_like(gsend)
    ncomp = ncell * B
    shape = (4, 128)
    row = lax.broadcasted_iota(jnp.int32, shape, 0)
    lane = lax.broadcasted_iota(jnp.int32, shape, 1)
    zero = jnp.zeros(shape, jnp.float32)
    loads[0].wait()

    packed_l, packed_r = zero, zero
    for k in range(ncomp):
        cell = k // B
        f_after = fv[0, k + B] if cell < ncell - 1 else zero
        f_before = fv[0, k - B] if cell > 0 else zero
        g = fv[1, k]
        h = fv[2, k]
        blank = jnp.zeros((1, 128), jnp.float32)
        dy = jnp.concatenate([g[1:], blank], 0) - jnp.concatenate([blank, g[:-1]], 0)
        h_after = jnp.where(lane == 127, 0.0, pltpu.roll(h, 127, 1))
        h_before = jnp.where(lane == 0, 0.0, pltpu.roll(h, 1, 1))
        rv[k] = -0.5 * ((f_after - f_before) + dy + (h_after - h_before))
        ysl[k : k + 1, :] = g[0:1]
        ysr[k : k + 1, :] = g[3:4]
        packed_l = jnp.where(lane == k, pltpu.roll(h, k, 1), packed_l)
        packed_r = jnp.where(lane == k, pltpu.roll(h, (k + 1) % 128, 1), packed_r)
    zsl[...] = packed_l
    zsr[...] = packed_r

    loads[1].wait()
    loads[2].wait()

    def first_level(j, carry):
        m = 2 * j + 1
        cut = jnp.logical_and(m == ncell - 1, p == n - 1)
        keep = jnp.where(cut, 0.0, 1.0)
        before = [jv[(m - 1) * B * B + i * B + k] for i, k in SYM]
        after = [jv[m * B * B + i * B + k] * keep for i, k in SYM]
        inv = 1.0 / (1.0 + dv[m])
        full_b = [[before[POS[i, k]] for k in range(B)] for i in range(B)]
        full_a = [[after[POS[i, k]] for k in range(B)] for i in range(B)]
        scaled_b = [[(before[POS[i, k]] * inv) for k in range(B)] for i in range(B)]
        scaled_a = [[(after[POS[i, k]] * inv) for k in range(B)] for i in range(B)]
        for e, value in enumerate(product_sym(full_b, scaled_b)):
            el[j * NMAT + GL + e] = value
        for e, value in enumerate(product_sym(full_a, scaled_a)):
            el[j * NMAT + GR + e] = value
        couple = product(full_a, scaled_b)
        for e in range(B * B):
            el[j * NMAT + CC + e] = couple[e // B][e % B]
        return carry

    lax.fori_loop(0, ncell // 2, first_level, 0)

    pl.semaphore_wait(barrier, len(peers) + 4 - solvers_here)

    halo = []

    def send_halo(src, dst, index, peer):
        copy = pltpu.make_async_remote_copy(
            src_ref=src,
            dst_ref=dst,
            send_sem=hsend.at[index],
            recv_sem=hrecv.at[index],
            device_id=peer,
            device_id_type=MESH,
        )
        copy.start()
        halo.append(copy)

    send_halo(fv.at[0, pl.ds(ncomp - B, B)], xl, 0, {"line": lax.rem(p + 1, n)})
    send_halo(fv.at[0, pl.ds(0, B)], xr, 1, {"line": lax.rem(p + n - 1, n)})
    send_halo(ysr, yl, 2, {"py": lax.rem(py + 1, npy)})
    send_halo(ysl, yr, 3, {"py": lax.rem(py + npy - 1, npy)})
    send_halo(zsr, zl, 4, {"pz": lax.rem(pz + 1, npz)})
    send_halo(zsl, zr, 5, {"pz": lax.rem(pz + npz - 1, npz)})

    def merge(i, carry):
        a, b, new = 2 * i * NMAT, (2 * i + 1) * NMAT, (4 + i) * NMAT
        m = jnp.where(i == 2, 4, 2 + 4 * i)
        pivot = [el[a + GR + e] + el[b + GL + e] for e in range(NSYM)]
        diag = 1.0 + dv[m]
        for k in range(B):
            pivot[POS[k, k]] = pivot[POS[k, k]] + diag
        inv = sym_inverse(pivot)
        ca = as_mat([el[a + CC + e] for e in range(B * B)])
        cb = as_mat([el[b + CC + e] for e in range(B * B)])
        w = sym_times(inv, ca)
        u = sym_times(inv, transposed(cb))
        gl_new = product_sym(transposed(ca), w)
        gr_new = product_sym(cb, u)
        c_new = product(cb, w)
        for e in range(NSYM):
            el[new + GL + e] = el[a + GL + e] - gl_new[e]
            el[new + GR + e] = el[b + GR + e] - gr_new[e]
            facs[i * 65 + e] = inv[e]
        for e in range(B * B):
            el[new + CC + e] = c_new[e // B][e % B]
            facs[i * 65 + NSYM + e] = w[e // B][e % B]
            facs[i * 65 + NSYM + B * B + e] = u[e // B][e % B]
        return carry

    lax.fori_loop(0, 3, merge, 0)

    diag0 = 1.0 + dv[0]
    for e in range(NMAT):
        value = el[6 * NMAT + e]
        if e < NSYM and SYM[e][0] == SYM[e][1]:
            value = value + diag0
        msend[pl.ds(e, 4, stride=MROWS), :] = value

    def part_copies(src, dst, rows, sent, send_sem, recv_sem, s):
        here = src.at[pl.ds(s * rows, sent)]
        there = dst.at[pl.ds(pl.multiple_of(p * rows, 8), sent)]
        away = pltpu.make_async_remote_copy(
            src_ref=here,
            dst_ref=there,
            send_sem=send_sem.at[s],
            recv_sem=recv_sem.at[p],
            device_id={"line": solver[s]},
            device_id_type=MESH,
        )
        return away, pltpu.make_async_copy(here, there, send_sem.at[s])

    def start_parts(src, dst, rows, sent, send_sem, recv_sem):
        for s in range(4):
            away, near = part_copies(src, dst, rows, sent, send_sem, recv_sem, s)
            pl.when(solver[s] != p)(away.start)
            pl.when(solver[s] == p)(near.start)

    def finish_parts(src, dst, rows, sent, send_sem, recv_sem):
        for s in range(4):
            away, near = part_copies(src, dst, rows, sent, send_sem, recv_sem, s)
            pl.when(solver[s] != p)(away.wait_send)
            pl.when(solver[s] == p)(near.wait)

    def await_parts(src, dst, rows, sent, send_sem, recv_sem):
        def one(q, carry):
            copy = pltpu.make_async_remote_copy(
                src_ref=src.at[pl.ds(0, sent)],
                dst_ref=dst.at[pl.ds(pl.multiple_of(q * rows, 8), sent)],
                send_sem=send_sem.at[0],
                recv_sem=recv_sem.at[q],
                device_id={"line": solver[0]},
                device_id_type=MESH,
            )
            pl.when(q != p)(copy.wait_recv)
            return carry

        lax.fori_loop(0, n, one, 0)

    mats = (msend, mrecv, MROWS, NMAT, m_s, m_r)
    sides = (gsend, grecv, GROWS, GSEND, g_s, g_r)
    start_parts(*mats)

    for copy in halo:
        copy.wait_recv()

    x_first = jnp.where(p > 0, 0.5, 0.0)
    x_last = jnp.where(p < n - 1, -0.5, 0.0)
    y_first = jnp.where(row == 0, jnp.where(py > 0, 0.5, 0.0), 0.0)
    y_last = jnp.where(row == 3, jnp.where(py < npy - 1, -0.5, 0.0), 0.0)
    z_first = jnp.where(lane == 0, jnp.where(pz > 0, 0.5, 0.0), 0.0)
    z_last = jnp.where(lane == 127, jnp.where(pz < npz - 1, -0.5, 0.0), 0.0)
    z_left, z_right = zl[...], zr[...]
    for k in range(ncomp):
        value = rv[k] + y_first * yl[k : k + 1, :] + y_last * yr[k : k + 1, :]
        value = value + z_first * pltpu.roll(z_left, (128 - k) % 128, 1)
        value = value + z_last * pltpu.roll(z_right, 127 - k, 1)
        if k < B:
            value = value + x_first * xl[k]
        if k >= ncomp - B:
            value = value + x_last * xr[k - ncomp + B]
        rv[k] = value

    def sym_face(f):
        return [jv[f * B * B + i * B + k] for i, k in SYM]

    keep_last = jnp.where(p == n - 1, 0.0, 1.0)
    g_left, g_right = [None] * 7, [None] * 7
    for j in range(ncell // 2):
        m = 2 * j + 1
        inv = 1.0 / (1.0 + dv[m])
        scaled = [rv[m * B + i] * inv for i in range(B)]
        g_left[j] = [-v for v in sym_vec(sym_face(m - 1), scaled)]
        after = scaled if m < ncell - 1 else [v * keep_last for v in scaled]
        g_right[j] = sym_vec(sym_face(m), after)
    for i, m in enumerate((2, 6, 4)):
        a, b = 2 * i, 2 * i + 1
        q = [rv[m * B + c] + g_right[a][c] + g_left[b][c] for c in range(B)]
        w = as_mat([facs[i * 65 + NSYM + e] for e in range(B * B)])
        u = as_mat([facs[i * 65 + NSYM + B * B + e] for e in range(B * B)])
        more_l = mat_vec(transposed(w), q)
        more_r = mat_vec(transposed(u), q)
        g_left[4 + i] = [g_left[a][c] + more_l[c] for c in range(B)]
        g_right[4 + i] = [g_right[b][c] + more_r[c] for c in range(B)]
        for c in range(B):
            gel[i * B + c] = q[c]
    for c in range(B):
        gsend[pl.ds(c, 4, stride=GROWS), :] = rv[c] + g_left[6][c]
        gsend[pl.ds(B + c, 4, stride=GROWS), :] = g_right[6][c]

    start_parts(*sides)
    for i in range(3):
        value = sym_vec([facs[i * 65 + e] for e in range(NSYM)], [gel[i * B + c] for c in range(B)])
        for c in range(B):
            yv[i * B + c] = value[c]

    def answer_copy(q):
        return pltpu.make_async_remote_copy(
            src_ref=sol.at[pl.ds(pl.multiple_of(q * 8, 8), 16)],
            dst_ref=xrecv.at[pl.ds(pl.multiple_of(mine * 16, 16), 16)],
            send_sem=x_s.at[q],
            recv_sem=x_r.at[mine],
            device_id={"line": q},
            device_id_type=MESH,
        )

    own_answer = pltpu.make_async_copy(
        sol.at[pl.ds(pl.multiple_of(p * 8, 8), 16)],
        xrecv.at[pl.ds(pl.multiple_of(mine * 16, 16), 16)],
        x_s.at[p],
    )

    def solve():
        finish_parts(*mats)
        await_parts(*mats)

        def even(e):
            return mrecv[pl.ds(e, 8, stride=2 * MROWS), :]

        def odd(e):
            return mrecv[pl.ds(MROWS + e, 8, stride=2 * MROWS), :]

        inv0 = sym_inverse([odd(GL + e) + even(GR + e) for e in range(NSYM)])
        ca = as_mat([even(CC + e) for e in range(B * B)])
        cb = as_mat([odd(CC + e) for e in range(B * B)])
        w0 = sym_times(inv0, ca)
        u0 = sym_times(inv0, transposed(cb))
        less_l = product_sym(transposed(ca), w0)
        less_r = product_sym(cb, u0)
        diag = [even(GL + e) - less_l[e] + pltpu.roll(odd(GR + e) - less_r[e], 1, 0) for e in range(NSYM)]
        couple = product(cb, w0)
        base = 0

        def keep(values):
            nonlocal base
            start = base
            for value in values:
                sfac[base] = value
                base += 1
            return start

        def flat(mat):
            return [entry for line in mat for entry in line]

        at_inv0, at_w0, at_u0 = keep(inv0), keep(flat(w0)), keep(flat(u0))
        levels = []
        for step in (1, 2, 4):
            inv = sym_inverse(diag)
            left = [[pltpu.roll(entry, step, 0) for entry in line] for line in couple]
            w = sym_times(inv, left)
            u = sym_times(inv, transposed(couple))
            levels.append((step, keep(flat(w)), keep(flat(u))))
            less_l = product_sym(transposed(left), w)
            less_r = product_sym(couple, u)
            diag = [
                diag[e] - pltpu.roll(less_l[e], 8 - step, 0) - pltpu.roll(less_r[e], step, 0)
                for e in range(NSYM)
            ]
            if step < 4:
                couple = [[pltpu.roll(v, 8 - step, 0) for v in line] for line in product(couple, w)]
        at_last = keep(sym_inverse(diag))

        finish_parts(*sides)
        await_parts(*sides)

        def saved(start, count):
            return [sfac[start + e] for e in range(count)]

        def even_side(e):
            return grecv[pl.ds(e, 8, stride=2 * GROWS), :]

        def odd_side(e):
            return grecv[pl.ds(GROWS + e, 8, stride=2 * GROWS), :]

        w0 = as_mat(saved(at_w0, B * B))
        u0 = as_mat(saved(at_u0, B * B))
        q = [odd_side(c) + even_side(B + c) for c in range(B)]
        more_l = mat_vec(transposed(w0), q)
        more_r = mat_vec(transposed(u0), q)
        side = [
            even_side(c) + more_l[c] + pltpu.roll(odd_side(B + c) + more_r[c], 1, 0) for c in range(B)
        ]
        for step, at_w, at_u in levels:
            more_l = mat_vec(transposed(as_mat(saved(at_w, B * B))), side)
            more_r = mat_vec(transposed(as_mat(saved(at_u, B * B))), side)
            side = [
                side[c] + pltpu.roll(more_l[c], 8 - step, 0) + pltpu.roll(more_r[c], step, 0)
                for c in range(B)
            ]
        x_even = sym_vec(saved(at_last, NSYM), side)
        x_next = [pltpu.roll(v, 7, 0) for v in x_even]
        own = sym_vec(saved(at_inv0, NSYM), q)
        from_l = mat_vec(w0, x_even)
        from_r = mat_vec(u0, x_next)
        for c in range(B):
            sol[pl.ds(c, 8, stride=16), :] = x_even[c]
            sol[pl.ds(8 + c, 8, stride=16), :] = own[c] + from_l[c] + from_r[c]

        def send_one(q, carry):
            pl.when(q != p)(answer_copy(q).start)
            return carry

        lax.fori_loop(0, n, send_one, 0)
        own_answer.start()
        own_answer.wait()

    pl.when(is_solver)(solve)

    for s in range(4):
        copy = pltpu.make_async_remote_copy(
            src_ref=sol.at[pl.ds(0, 16)],
            dst_ref=xrecv.at[pl.ds(s * 16, 16)],
            send_sem=x_s.at[0],
            recv_sem=x_r.at[s],
            device_id={"line": solver[s]},
            device_id_type=MESH,
        )
        pl.when(solver[s] != p)(copy.wait_recv)

    x = [None] * (ncell + 1)
    x[0] = [xrecv[pl.ds(c, 4, stride=16), :] for c in range(B)]
    x[ncell] = [xrecv[pl.ds(8 + c, 4, stride=16), :] for c in range(B)]
    for i, (m, a, b) in ((2, (4, 0, 8)), (0, (2, 0, 4)), (1, (6, 4, 8))):
        w = as_mat([facs[i * 65 + NSYM + e] for e in range(B * B)])
        u = as_mat([facs[i * 65 + NSYM + B * B + e] for e in range(B * B)])
        from_l, from_r = mat_vec(w, x[a]), mat_vec(u, x[b])
        x[m] = [yv[i * B + c] + from_l[c] + from_r[c] for c in range(B)]
    for m in range(1, ncell, 2):
        inv = 1.0 / (1.0 + dv[m])
        from_l = sym_vec(sym_face(m - 1), x[m - 1])
        after = x[m + 1] if m < ncell - 1 else [v * keep_last for v in x[m + 1]]
        from_r = sym_vec(sym_face(m), after)
        x[m] = [(rv[m * B + c] + from_l[c] - from_r[c]) * inv for c in range(B)]
    for m in range(ncell):
        for c in range(B):
            out_ref[m * B + c] = x[m][c]

    for copy in halo:
        copy.wait_send()

    def others():
        finish_parts(*mats)
        finish_parts(*sides)

    pl.when(jnp.logical_not(is_solver))(others)

    def answers_sent():
        def one(q, carry):
            pl.when(q != p)(answer_copy(q).wait_send)
            return carry

        lax.fori_loop(0, n, one, 0)

    pl.when(is_solver)(answers_sent)


def per_device(sizes, fluxes, jacobian, dissipation):
    n, npy, npz = sizes
    ncell = jacobian.shape[0]
    tail = jacobian.shape[3:]
    f32 = jnp.float32
    vmem, dma = pltpu.VMEM, pltpu.SemaphoreType.DMA
    tile = lambda count: vmem((count,) + tail, f32)
    flat = lambda rows: vmem((rows, 128), f32)
    ncomp = ncell * B
    out = pl.pallas_call(
        functools.partial(kernel, n, npy, npz),
        out_shape=jax.ShapeDtypeStruct((ncomp,) + tail, f32),
        in_specs=[pl.BlockSpec(memory_space=pl.ANY)] * 3,
        out_specs=pl.BlockSpec(memory_space=pltpu.VMEM),
        scratch_shapes=[
            vmem((3, ncomp) + tail, f32),
            tile(ncell * B * B),
            tile(ncell),
            tile(B),
            tile(B),
            flat(ncomp),
            flat(ncomp),
            vmem(tail, f32),
            vmem(tail, f32),
            flat(ncomp),
            flat(ncomp),
            vmem(tail, f32),
            vmem(tail, f32),
            tile(ncomp),
            tile(7 * NMAT),
            tile(3 * 65),
            tile(3 * B),
            tile(3 * B),
            flat(4 * MROWS),
            flat(n * MROWS),
            flat(4 * GROWS),
            flat(n * GROWS),
            vmem((256, 8, 128), f32),
            flat((n + 1) * 8),
            flat(4 * 16),
            dma((3,)),
            dma((6,)),
            dma((6,)),
            dma((4,)),
            dma((n,)),
            dma((4,)),
            dma((n,)),
            dma((n,)),
            dma((4,)),
        ],
        compiler_params=pltpu.CompilerParams(
            collective_id=0, has_side_effects=True, vmem_limit_bytes=60 * 1024 * 1024
        ),
    )(
        fluxes.reshape((3, ncomp) + tail),
        jacobian.reshape((ncell * B * B,) + tail),
        dissipation,
    )
    return out.reshape((ncell, B) + tail)


def solution(mesh):
    sizes = tuple(mesh.shape[name] for name in ("line", "py", "pz"))
    return jax.shard_map(
        functools.partial(per_device, sizes),
        mesh=mesh,
        in_specs=(
            P(None, "line", None, "py", "pz"),
            P("line", None, None, "py", "pz"),
            P("line", "py", "pz"),
        ),
        out_specs=P("line", None, "py", "pz"),
        check_vma=False,
    )
```

```python
import functools

import jax
import jax.numpy as jnp
from jax import lax
from jax.experimental import pallas as pl
from jax.experimental.pallas import tpu as pltpu
from jax.sharding import PartitionSpec as P

MESH = pl.DeviceIdType.MESH
B = 5
SYM = [(i, j) for i in range(B) for j in range(i, B)]
POS = {}
for _n, (_i, _j) in enumerate(SYM):
    POS[_i, _j] = POS[_j, _i] = _n
NSYM = len(SYM)
GL, GR, CC = 0, NSYM, 2 * NSYM
NMAT = 2 * NSYM + B * B
MROWS = 56
SOLVERS = ((12, 13, 14, 15), (1, 3, 5, 7))
GROWS = 16
GSEND = 2 * B


def total(terms):
    result = terms[0]
    for term in terms[1:]:
        result = result + term
    return result


def sym_inverse(a):
    a = list(a)
    for k in range(B):
        scaling = 1.0 / a[POS[k, k]]
        col = {i: a[POS[i, k]] for i in range(B) if i != k}
        scaled = {i: col[i] * scaling for i in col}
        for i, j in SYM:
            if i != k and j != k:
                a[POS[i, j]] = a[POS[i, j]] - scaled[i] * col[j]
        for i in col:
            a[POS[i, k]] = scaled[i]
        a[POS[k, k]] = -scaling
    return [-entry for entry in a]


def sym_times(inv, mat):
    return [[total([inv[POS[i, k]] * mat[k][j] for k in range(B)]) for j in range(B)] for i in range(B)]


def mat_vec(mat, vec):
    return [total([mat[i][k] * vec[k] for k in range(B)]) for i in range(B)]


def sym_vec(mat, vec):
    return [total([mat[POS[i, k]] * vec[k] for k in range(B)]) for i in range(B)]


def transposed(mat):
    return [[mat[j][i] for j in range(B)] for i in range(B)]


def product_sym(left, right):
    return [total([left[i][k] * right[k][j] for k in range(B)]) for i, j in SYM]


def product(left, right):
    return [[total([left[i][k] * right[k][j] for k in range(B)]) for j in range(B)] for i in range(B)]


def as_mat(flat):
    return [[flat[i * B + j] for j in range(B)] for i in range(B)]


def kernel(
    n,
    npy,
    npz,
    flux_hbm,
    jac_hbm,
    diss_hbm,
    out_ref,
    fv,
    jv,
    dv,
    xl,
    xr,
    yl,
    yr,
    zl,
    zr,
    ysl,
    ysr,
    zsl,
    zsr,
    rv,
    el,
    facs,
    gel,
    yv,
    msend,
    mrecv,
    gsend,
    grecv,
    sfac,
    sol,
    xrecv,
    lsem,
    hsend,
    hrecv,
    m_s,
    m_r,
    g_s,
    g_r,
    x_s,
    x_r,
):
    p = lax.axis_index("line")
    py = lax.axis_index("py")
    pz = lax.axis_index("pz")
    core = lax.rem(py, 2)
    ncell = jv.shape[0] // (B * B)
    solver = [jnp.where(core == 0, SOLVERS[0][s], SOLVERS[1][s]) for s in range(4)]
    mine = sum(jnp.where(p == solver[s], s, 0) for s in range(4))
    solvers_here = sum(jnp.where(p == solver[s], 1, 0) for s in range(4))
    is_solver = solvers_here > 0

    barrier = pltpu.get_barrier_semaphore()
    peers = [{"line": lax.rem(p + o, n)} for o in (1, n - 1)]
    peers += [{"py": lax.rem(py + o, npy)} for o in (1, npy - 1)]
    peers += [{"pz": lax.rem(pz + o, npz)} for o in (1, npz - 1)]
    def greet_line():
        for t in range(1, n):
            far = {"line": lax.rem(p + n // 2 + (t // 2 if t % 2 else n - t // 2), n)}
            pl.semaphore_signal(barrier, inc=1, device_id=far, device_id_type=MESH)

    pl.when(is_solver)(greet_line)
    for peer in peers:
        pl.semaphore_signal(barrier, inc=1, device_id=peer, device_id_type=MESH)

    loads = [
        pltpu.make_async_copy(flux_hbm, fv, lsem.at[0]),
        pltpu.make_async_copy(jac_hbm, jv, lsem.at[1]),
        pltpu.make_async_copy(diss_hbm, dv, lsem.at[2]),
    ]
    for load in loads:
        load.start()
    msend[...] = jnp.zeros_like(msend)
    gsend[...] = jnp.zeros_like(gsend)
    ncomp = ncell * B
    shape = (4, 128)
    row = lax.broadcasted_iota(jnp.int32, shape, 0)
    lane = lax.broadcasted_iota(jnp.int32, shape, 1)
    zero = jnp.zeros(shape, jnp.float32)
    loads[0].wait()

    packed_l, packed_r = zero, zero
    for k in range(ncomp):
        cell = k // B
        f_after = fv[0, k + B] if cell < ncell - 1 else zero
        f_before = fv[0, k - B] if cell > 0 else zero
        g = fv[1, k]
        h = fv[2, k]
        blank = jnp.zeros((1, 128), jnp.float32)
        dy = jnp.concatenate([g[1:], blank], 0) - jnp.concatenate([blank, g[:-1]], 0)
        h_after = jnp.where(lane == 127, 0.0, pltpu.roll(h, 127, 1))
        h_before = jnp.where(lane == 0, 0.0, pltpu.roll(h, 1, 1))
        rv[k] = -0.5 * ((f_after - f_before) + dy + (h_after - h_before))
        ysl[k : k + 1, :] = g[0:1]
        ysr[k : k + 1, :] = g[3:4]
        packed_l = jnp.where(lane == k, pltpu.roll(h, k, 1), packed_l)
        packed_r = jnp.where(lane == k, pltpu.roll(h, (k + 1) % 128, 1), packed_r)
    zsl[...] = packed_l
    zsr[...] = packed_r

    loads[1].wait()
    loads[2].wait()

    def first_level(j, carry):
        m = 2 * j + 1
        cut = jnp.logical_and(m == ncell - 1, p == n - 1)
        keep = jnp.where(cut, 0.0, 1.0)
        before = [jv[(m - 1) * B * B + i * B + k] for i, k in SYM]
        after = [jv[m * B * B + i * B + k] * keep for i, k in SYM]
        inv = 1.0 / (1.0 + dv[m])
        full_b = [[before[POS[i, k]] for k in range(B)] for i in range(B)]
        full_a = [[after[POS[i, k]] for k in range(B)] for i in range(B)]
        scaled_b = [[(before[POS[i, k]] * inv) for k in range(B)] for i in range(B)]
        scaled_a = [[(after[POS[i, k]] * inv) for k in range(B)] for i in range(B)]
        for e, value in enumerate(product_sym(full_b, scaled_b)):
            el[j * NMAT + GL + e] = value
        for e, value in enumerate(product_sym(full_a, scaled_a)):
            el[j * NMAT + GR + e] = value
        couple = product(full_a, scaled_b)
        for e in range(B * B):
            el[j * NMAT + CC + e] = couple[e // B][e % B]
        return carry

    lax.fori_loop(0, ncell // 2, first_level, 0)

    def merge(i, carry):
        a, b, new = 2 * i * NMAT, (2 * i + 1) * NMAT, (4 + i) * NMAT
        m = jnp.where(i == 2, 4, 2 + 4 * i)
        pivot = [el[a + GR + e] + el[b + GL + e] for e in range(NSYM)]
        diag = 1.0 + dv[m]
        for k in range(B):
            pivot[POS[k, k]] = pivot[POS[k, k]] + diag
        inv = sym_inverse(pivot)
        ca = as_mat([el[a + CC + e] for e in range(B * B)])
        cb = as_mat([el[b + CC + e] for e in range(B * B)])
        w = sym_times(inv, ca)
        u = sym_times(inv, transposed(cb))
        gl_new = product_sym(transposed(ca), w)
        gr_new = product_sym(cb, u)
        c_new = product(cb, w)
        for e in range(NSYM):
            el[new + GL + e] = el[a + GL + e] - gl_new[e]
            el[new + GR + e] = el[b + GR + e] - gr_new[e]
            facs[i * 65 + e] = inv[e]
        for e in range(B * B):
            el[new + CC + e] = c_new[e // B][e % B]
            facs[i * 65 + NSYM + e] = w[e // B][e % B]
            facs[i * 65 + NSYM + B * B + e] = u[e // B][e % B]
        return carry

    lax.fori_loop(0, 3, merge, 0)

    diag0 = 1.0 + dv[0]
    for e in range(NMAT):
        value = el[6 * NMAT + e]
        if e < NSYM and SYM[e][0] == SYM[e][1]:
            value = value + diag0
        msend[pl.ds(e, 4, stride=MROWS), :] = value

    pl.semaphore_wait(barrier, len(peers) + 4 - solvers_here)

    halo = []

    def send_halo(src, dst, index, peer):
        copy = pltpu.make_async_remote_copy(
            src_ref=src,
            dst_ref=dst,
            send_sem=hsend.at[index],
            recv_sem=hrecv.at[index],
            device_id=peer,
            device_id_type=MESH,
        )
        copy.start()
        halo.append(copy)

    send_halo(fv.at[0, pl.ds(ncomp - B, B)], xl, 0, {"line": lax.rem(p + 1, n)})
    send_halo(fv.at[0, pl.ds(0, B)], xr, 1, {"line": lax.rem(p + n - 1, n)})
    send_halo(ysr, yl, 2, {"py": lax.rem(py + 1, npy)})
    send_halo(ysl, yr, 3, {"py": lax.rem(py + npy - 1, npy)})
    send_halo(zsr, zl, 4, {"pz": lax.rem(pz + 1, npz)})
    send_halo(zsl, zr, 5, {"pz": lax.rem(pz + npz - 1, npz)})

    def part_copies(src, dst, rows, sent, send_sem, recv_sem, s):
        here = src.at[pl.ds(s * rows, sent)]
        there = dst.at[pl.ds(pl.multiple_of(p * rows, 8), sent)]
        away = pltpu.make_async_remote_copy(
            src_ref=here,
            dst_ref=there,
            send_sem=send_sem.at[s],
            recv_sem=recv_sem.at[p],
            device_id={"line": solver[s]},
            device_id_type=MESH,
        )
        return away, pltpu.make_async_copy(here, there, send_sem.at[s])

    def start_parts(src, dst, rows, sent, send_sem, recv_sem):
        for s in range(4):
            away, near = part_copies(src, dst, rows, sent, send_sem, recv_sem, s)
            pl.when(solver[s] != p)(away.start)
            pl.when(solver[s] == p)(near.start)

    def finish_parts(src, dst, rows, sent, send_sem, recv_sem):
        for s in range(4):
            away, near = part_copies(src, dst, rows, sent, send_sem, recv_sem, s)
            pl.when(solver[s] != p)(away.wait_send)
            pl.when(solver[s] == p)(near.wait)

    def await_parts(src, dst, rows, sent, send_sem, recv_sem):
        def one(q, carry):
            copy = pltpu.make_async_remote_copy(
                src_ref=src.at[pl.ds(0, sent)],
                dst_ref=dst.at[pl.ds(pl.multiple_of(q * rows, 8), sent)],
                send_sem=send_sem.at[0],
                recv_sem=recv_sem.at[q],
                device_id={"line": solver[0]},
                device_id_type=MESH,
            )
            pl.when(q != p)(copy.wait_recv)
            return carry

        lax.fori_loop(0, n, one, 0)

    mats = (msend, mrecv, MROWS, NMAT, m_s, m_r)
    sides = (gsend, grecv, GROWS, GSEND, g_s, g_r)
    start_parts(*mats)

    for copy in halo:
        copy.wait_recv()

    x_first = jnp.where(p > 0, 0.5, 0.0)
    x_last = jnp.where(p < n - 1, -0.5, 0.0)
    y_first = jnp.where(row == 0, jnp.where(py > 0, 0.5, 0.0), 0.0)
    y_last = jnp.where(row == 3, jnp.where(py < npy - 1, -0.5, 0.0), 0.0)
    z_first = jnp.where(lane == 0, jnp.where(pz > 0, 0.5, 0.0), 0.0)
    z_last = jnp.where(lane == 127, jnp.where(pz < npz - 1, -0.5, 0.0), 0.0)
    z_left, z_right = zl[...], zr[...]
    for k in range(ncomp):
        value = rv[k] + y_first * yl[k : k + 1, :] + y_last * yr[k : k + 1, :]
        value = value + z_first * pltpu.roll(z_left, (128 - k) % 128, 1)
        value = value + z_last * pltpu.roll(z_right, 127 - k, 1)
        if k < B:
            value = value + x_first * xl[k]
        if k >= ncomp - B:
            value = value + x_last * xr[k - ncomp + B]
        rv[k] = value

    def sym_face(f):
        return [jv[f * B * B + i * B + k] for i, k in SYM]

    keep_last = jnp.where(p == n - 1, 0.0, 1.0)
    g_left, g_right = [None] * 7, [None] * 7
    for j in range(ncell // 2):
        m = 2 * j + 1
        inv = 1.0 / (1.0 + dv[m])
        scaled = [rv[m * B + i] * inv for i in range(B)]
        g_left[j] = [-v for v in sym_vec(sym_face(m - 1), scaled)]
        after = scaled if m < ncell - 1 else [v * keep_last for v in scaled]
        g_right[j] = sym_vec(sym_face(m), after)
    for i, m in enumerate((2, 6, 4)):
        a, b = 2 * i, 2 * i + 1
        q = [rv[m * B + c] + g_right[a][c] + g_left[b][c] for c in range(B)]
        w = as_mat([facs[i * 65 + NSYM + e] for e in range(B * B)])
        u = as_mat([facs[i * 65 + NSYM + B * B + e] for e in range(B * B)])
        more_l = mat_vec(transposed(w), q)
        more_r = mat_vec(transposed(u), q)
        g_left[4 + i] = [g_left[a][c] + more_l[c] for c in range(B)]
        g_right[4 + i] = [g_right[b][c] + more_r[c] for c in range(B)]
        for c in range(B):
            gel[i * B + c] = q[c]
    for c in range(B):
        gsend[pl.ds(c, 4, stride=GROWS), :] = rv[c] + g_left[6][c]
        gsend[pl.ds(B + c, 4, stride=GROWS), :] = g_right[6][c]

    start_parts(*sides)
    for i in range(3):
        value = sym_vec([facs[i * 65 + e] for e in range(NSYM)], [gel[i * B + c] for c in range(B)])
        for c in range(B):
            yv[i * B + c] = value[c]

    def answer_copy(q):
        return pltpu.make_async_remote_copy(
            src_ref=sol.at[pl.ds(pl.multiple_of(q * GROWS, 16), GSEND)],
            dst_ref=xrecv.at[pl.ds(pl.multiple_of(mine * GROWS, 16), GSEND)],
            send_sem=x_s.at[q],
            recv_sem=x_r.at[mine],
            device_id={"line": q},
            device_id_type=MESH,
        )

    own_answer = pltpu.make_async_copy(
        sol.at[pl.ds(pl.multiple_of(p * GROWS, 16), GSEND)],
        xrecv.at[pl.ds(pl.multiple_of(mine * GROWS, 16), GSEND)],
        x_s.at[p],
    )

    def solve():
        finish_parts(*mats)
        await_parts(*mats)

        def even(e):
            return mrecv[pl.ds(e, 8, stride=2 * MROWS), :]

        def odd(e):
            return mrecv[pl.ds(MROWS + e, 8, stride=2 * MROWS), :]

        inv0 = sym_inverse([odd(GL + e) + even(GR + e) for e in range(NSYM)])
        ca = as_mat([even(CC + e) for e in range(B * B)])
        cb = as_mat([odd(CC + e) for e in range(B * B)])
        w0 = sym_times(inv0, ca)
        u0 = sym_times(inv0, transposed(cb))
        less_l = product_sym(transposed(ca), w0)
        less_r = product_sym(cb, u0)
        diag = [even(GL + e) - less_l[e] + pltpu.roll(odd(GR + e) - less_r[e], 1, 0) for e in range(NSYM)]
        couple = product(cb, w0)
        base = 0

        def keep(values):
            nonlocal base
            start = base
            for value in values:
                sfac[base] = value
                base += 1
            return start

        def flat(mat):
            return [entry for line in mat for entry in line]

        at_inv0, at_w0, at_u0 = keep(inv0), keep(flat(w0)), keep(flat(u0))
        levels = []
        for step in (1, 2, 4):
            inv = sym_inverse(diag)
            left = [[pltpu.roll(entry, step, 0) for entry in line] for line in couple]
            w = sym_times(inv, left)
            u = sym_times(inv, transposed(couple))
            levels.append((step, keep(flat(w)), keep(flat(u))))
            less_l = product_sym(transposed(left), w)
            less_r = product_sym(couple, u)
            diag = [
                diag[e] - pltpu.roll(less_l[e], 8 - step, 0) - pltpu.roll(less_r[e], step, 0)
                for e in range(NSYM)
            ]
            if step < 4:
                couple = [[pltpu.roll(v, 8 - step, 0) for v in line] for line in product(couple, w)]
        at_last = keep(sym_inverse(diag))

        finish_parts(*sides)
        await_parts(*sides)

        def saved(start, count):
            return [sfac[start + e] for e in range(count)]

        def even_side(e):
            return grecv[pl.ds(e, 8, stride=2 * GROWS), :]

        def odd_side(e):
            return grecv[pl.ds(GROWS + e, 8, stride=2 * GROWS), :]

        w0 = as_mat(saved(at_w0, B * B))
        u0 = as_mat(saved(at_u0, B * B))
        q = [odd_side(c) + even_side(B + c) for c in range(B)]
        more_l = mat_vec(transposed(w0), q)
        more_r = mat_vec(transposed(u0), q)
        side = [
            even_side(c) + more_l[c] + pltpu.roll(odd_side(B + c) + more_r[c], 1, 0) for c in range(B)
        ]
        for step, at_w, at_u in levels:
            more_l = mat_vec(transposed(as_mat(saved(at_w, B * B))), side)
            more_r = mat_vec(transposed(as_mat(saved(at_u, B * B))), side)
            side = [
                side[c] + pltpu.roll(more_l[c], 8 - step, 0) + pltpu.roll(more_r[c], step, 0)
                for c in range(B)
            ]
        x_even = sym_vec(saved(at_last, NSYM), side)
        x_next = [pltpu.roll(v, 7, 0) for v in x_even]
        own = sym_vec(saved(at_inv0, NSYM), q)
        from_l = mat_vec(w0, x_even)
        from_r = mat_vec(u0, x_next)
        for c in range(B):
            x_odd = own[c] + from_l[c] + from_r[c]
            sol[pl.ds(c, 8, stride=2 * GROWS), :] = x_even[c]
            sol[pl.ds(B + c, 8, stride=2 * GROWS), :] = x_odd
            sol[pl.ds(GROWS + c, 8, stride=2 * GROWS), :] = x_odd
            sol[pl.ds(GROWS + B + c, 8, stride=2 * GROWS), :] = x_next[c]

        def send_one(q, carry):
            pl.when(q != p)(answer_copy(q).start)
            return carry

        lax.fori_loop(0, n, send_one, 0)
        own_answer.start()
        own_answer.wait()

    pl.when(is_solver)(solve)

    for s in range(4):
        copy = pltpu.make_async_remote_copy(
            src_ref=sol.at[pl.ds(0, GSEND)],
            dst_ref=xrecv.at[pl.ds(s * GROWS, GSEND)],
            send_sem=x_s.at[0],
            recv_sem=x_r.at[s],
            device_id={"line": solver[s]},
            device_id_type=MESH,
        )
        pl.when(solver[s] != p)(copy.wait_recv)

    x = [None] * (ncell + 1)
    x[0] = [xrecv[pl.ds(c, 4, stride=GROWS), :] for c in range(B)]
    x[ncell] = [xrecv[pl.ds(B + c, 4, stride=GROWS), :] for c in range(B)]
    for i, (m, a, b) in ((2, (4, 0, 8)), (0, (2, 0, 4)), (1, (6, 4, 8))):
        w = as_mat([facs[i * 65 + NSYM + e] for e in range(B * B)])
        u = as_mat([facs[i * 65 + NSYM + B * B + e] for e in range(B * B)])
        from_l, from_r = mat_vec(w, x[a]), mat_vec(u, x[b])
        x[m] = [yv[i * B + c] + from_l[c] + from_r[c] for c in range(B)]
    for m in range(1, ncell, 2):
        inv = 1.0 / (1.0 + dv[m])
        from_l = sym_vec(sym_face(m - 1), x[m - 1])
        after = x[m + 1] if m < ncell - 1 else [v * keep_last for v in x[m + 1]]
        from_r = sym_vec(sym_face(m), after)
        x[m] = [(rv[m * B + c] + from_l[c] - from_r[c]) * inv for c in range(B)]
    for m in range(ncell):
        for c in range(B):
            out_ref[m * B + c] = x[m][c]

    for copy in halo:
        copy.wait_send()

    def others():
        finish_parts(*mats)
        finish_parts(*sides)

    pl.when(jnp.logical_not(is_solver))(others)

    def answers_sent():
        def one(q, carry):
            pl.when(q != p)(answer_copy(q).wait_send)
            return carry

        lax.fori_loop(0, n, one, 0)

    pl.when(is_solver)(answers_sent)


def per_device(sizes, fluxes, jacobian, dissipation):
    n, npy, npz = sizes
    ncell = jacobian.shape[0]
    tail = jacobian.shape[3:]
    f32 = jnp.float32
    vmem, dma = pltpu.VMEM, pltpu.SemaphoreType.DMA
    tile = lambda count: vmem((count,) + tail, f32)
    flat = lambda rows: vmem((rows, 128), f32)
    ncomp = ncell * B
    out = pl.pallas_call(
        functools.partial(kernel, n, npy, npz),
        out_shape=jax.ShapeDtypeStruct((ncomp,) + tail, f32),
        in_specs=[pl.BlockSpec(memory_space=pl.ANY)] * 3,
        out_specs=pl.BlockSpec(memory_space=pltpu.VMEM),
        scratch_shapes=[
            vmem((3, ncomp) + tail, f32),
            tile(ncell * B * B),
            tile(ncell),
            tile(B),
            tile(B),
            flat(ncomp),
            flat(ncomp),
            vmem(tail, f32),
            vmem(tail, f32),
            flat(ncomp),
            flat(ncomp),
            vmem(tail, f32),
            vmem(tail, f32),
            tile(ncomp),
            tile(7 * NMAT),
            tile(3 * 65),
            tile(3 * B),
            tile(3 * B),
            flat(4 * MROWS),
            flat(n * MROWS),
            flat(4 * GROWS),
            flat(n * GROWS),
            vmem((256, 8, 128), f32),
            flat(n * GROWS),
            flat(4 * GROWS),
            dma((3,)),
            dma((6,)),
            dma((6,)),
            dma((4,)),
            dma((n,)),
            dma((4,)),
            dma((n,)),
            dma((n,)),
            dma((4,)),
        ],
        compiler_params=pltpu.CompilerParams(
            collective_id=0, has_side_effects=True, vmem_limit_bytes=60 * 1024 * 1024
        ),
    )(
        fluxes.reshape((3, ncomp) + tail),
        jacobian.reshape((ncell * B * B,) + tail),
        dissipation,
    )
    return out.reshape((ncell, B) + tail)


def solution(mesh):
    sizes = tuple(mesh.shape[name] for name in ("line", "py", "pz"))
    return jax.shard_map(
        functools.partial(per_device, sizes),
        mesh=mesh,
        in_specs=(
            P(None, "line", None, "py", "pz"),
            P("line", None, None, "py", "pz"),
            P("line", "py", "pz"),
        ),
        out_specs=P("line", None, "py", "pz"),
        check_vma=False,
    )
```

```python
import functools

import jax
import jax.numpy as jnp
from jax import lax
from jax.experimental import pallas as pl
from jax.experimental.pallas import tpu as pltpu
from jax.sharding import PartitionSpec as P

MESH = pl.DeviceIdType.MESH
B = 5
SYM = [(i, j) for i in range(B) for j in range(i, B)]
POS = {}
for _n, (_i, _j) in enumerate(SYM):
    POS[_i, _j] = POS[_j, _i] = _n
NSYM = len(SYM)
GL, GR, CC = 0, NSYM, 2 * NSYM
NMAT = 2 * NSYM + B * B
MROWS = 56
SOLVERS = ((12, 13, 14, 15), (1, 2, 3, 4))
GROWS = 16
GSEND = 2 * B


def total(terms):
    result = terms[0]
    for term in terms[1:]:
        result = result + term
    return result


def sym_inverse(a):
    a = list(a)
    for k in range(B):
        scaling = 1.0 / a[POS[k, k]]
        col = {i: a[POS[i, k]] for i in range(B) if i != k}
        scaled = {i: col[i] * scaling for i in col}
        for i, j in SYM:
            if i != k and j != k:
                a[POS[i, j]] = a[POS[i, j]] - scaled[i] * col[j]
        for i in col:
            a[POS[i, k]] = scaled[i]
        a[POS[k, k]] = -scaling
    return [-entry for entry in a]


def sym_times(inv, mat):
    return [[total([inv[POS[i, k]] * mat[k][j] for k in range(B)]) for j in range(B)] for i in range(B)]


def mat_vec(mat, vec):
    return [total([mat[i][k] * vec[k] for k in range(B)]) for i in range(B)]


def sym_vec(mat, vec):
    return [total([mat[POS[i, k]] * vec[k] for k in range(B)]) for i in range(B)]


def transposed(mat):
    return [[mat[j][i] for j in range(B)] for i in range(B)]


def product_sym(left, right):
    return [total([left[i][k] * right[k][j] for k in range(B)]) for i, j in SYM]


def product(left, right):
    return [[total([left[i][k] * right[k][j] for k in range(B)]) for j in range(B)] for i in range(B)]


def as_mat(flat):
    return [[flat[i * B + j] for j in range(B)] for i in range(B)]


def kernel(
    n,
    npy,
    npz,
    flux_hbm,
    jac_hbm,
    diss_hbm,
    out_ref,
    fv,
    jv,
    dv,
    xl,
    xr,
    yl,
    yr,
    zl,
    zr,
    ysl,
    ysr,
    zsl,
    zsr,
    rv,
    el,
    facs,
    gel,
    yv,
    msend,
    mrecv,
    gsend,
    grecv,
    sfac,
    sol,
    xrecv,
    lsem,
    hsend,
    hrecv,
    m_s,
    m_r,
    g_s,
    g_r,
    x_s,
    x_r,
):
    p = lax.axis_index("line")
    py = lax.axis_index("py")
    pz = lax.axis_index("pz")
    core = lax.rem(py, 2)
    ncell = jv.shape[0] // (B * B)
    solver = [jnp.where(core == 0, SOLVERS[0][s], SOLVERS[1][s]) for s in range(4)]
    mine = sum(jnp.where(p == solver[s], s, 0) for s in range(4))
    solvers_here = sum(jnp.where(p == solver[s], 1, 0) for s in range(4))
    is_solver = solvers_here > 0

    barrier = pltpu.get_barrier_semaphore()
    peers = [{"line": lax.rem(p + o, n)} for o in (1, n - 1)]
    peers += [{"py": lax.rem(py + o, npy)} for o in (1, npy - 1)]
    peers += [{"pz": lax.rem(pz + o, npz)} for o in (1, npz - 1)]
    def greet_line():
        for t in range(1, n):
            far = {"line": lax.rem(p + n // 2 + (t // 2 if t % 2 else n - t // 2), n)}
            pl.semaphore_signal(barrier, inc=1, device_id=far, device_id_type=MESH)

    pl.when(is_solver)(greet_line)
    for peer in peers:
        pl.semaphore_signal(barrier, inc=1, device_id=peer, device_id_type=MESH)

    loads = [
        pltpu.make_async_copy(flux_hbm, fv, lsem.at[0]),
        pltpu.make_async_copy(jac_hbm, jv, lsem.at[1]),
        pltpu.make_async_copy(diss_hbm, dv, lsem.at[2]),
    ]
    for load in loads:
        load.start()
    msend[...] = jnp.zeros_like(msend)
    gsend[...] = jnp.zeros_like(gsend)
    ncomp = ncell * B
    shape = (4, 128)
    row = lax.broadcasted_iota(jnp.int32, shape, 0)
    lane = lax.broadcasted_iota(jnp.int32, shape, 1)
    zero = jnp.zeros(shape, jnp.float32)
    loads[0].wait()

    packed_l, packed_r = zero, zero
    for k in range(ncomp):
        cell = k // B
        f_after = fv[0, k + B] if cell < ncell - 1 else zero
        f_before = fv[0, k - B] if cell > 0 else zero
        g = fv[1, k]
        h = fv[2, k]
        blank = jnp.zeros((1, 128), jnp.float32)
        dy = jnp.concatenate([g[1:], blank], 0) - jnp.concatenate([blank, g[:-1]], 0)
        h_after = jnp.where(lane == 127, 0.0, pltpu.roll(h, 127, 1))
        h_before = jnp.where(lane == 0, 0.0, pltpu.roll(h, 1, 1))
        rv[k] = -0.5 * ((f_after - f_before) + dy + (h_after - h_before))
        ysl[k : k + 1, :] = g[0:1]
        ysr[k : k + 1, :] = g[3:4]
        packed_l = jnp.where(lane == k, pltpu.roll(h, k, 1), packed_l)
        packed_r = jnp.where(lane == k, pltpu.roll(h, (k + 1) % 128, 1), packed_r)
    zsl[...] = packed_l
    zsr[...] = packed_r

    loads[1].wait()
    loads[2].wait()

    def first_level(j, carry):
        m = 2 * j + 1
        cut = jnp.logical_and(m == ncell - 1, p == n - 1)
        keep = jnp.where(cut, 0.0, 1.0)
        before = [jv[(m - 1) * B * B + i * B + k] for i, k in SYM]
        after = [jv[m * B * B + i * B + k] * keep for i, k in SYM]
        inv = 1.0 / (1.0 + dv[m])
        full_b = [[before[POS[i, k]] for k in range(B)] for i in range(B)]
        full_a = [[after[POS[i, k]] for k in range(B)] for i in range(B)]
        scaled_b = [[(before[POS[i, k]] * inv) for k in range(B)] for i in range(B)]
        scaled_a = [[(after[POS[i, k]] * inv) for k in range(B)] for i in range(B)]
        for e, value in enumerate(product_sym(full_b, scaled_b)):
            el[j * NMAT + GL + e] = value
        for e, value in enumerate(product_sym(full_a, scaled_a)):
            el[j * NMAT + GR + e] = value
        couple = product(full_a, scaled_b)
        for e in range(B * B):
            el[j * NMAT + CC + e] = couple[e // B][e % B]
        return carry

    lax.fori_loop(0, ncell // 2, first_level, 0)

    def merge(i, carry):
        a, b, new = 2 * i * NMAT, (2 * i + 1) * NMAT, (4 + i) * NMAT
        m = jnp.where(i == 2, 4, 2 + 4 * i)
        pivot = [el[a + GR + e] + el[b + GL + e] for e in range(NSYM)]
        diag = 1.0 + dv[m]
        for k in range(B):
            pivot[POS[k, k]] = pivot[POS[k, k]] + diag
        inv = sym_inverse(pivot)
        ca = as_mat([el[a + CC + e] for e in range(B * B)])
        cb = as_mat([el[b + CC + e] for e in range(B * B)])
        w = sym_times(inv, ca)
        u = sym_times(inv, transposed(cb))
        gl_new = product_sym(transposed(ca), w)
        gr_new = product_sym(cb, u)
        c_new = product(cb, w)
        for e in range(NSYM):
            el[new + GL + e] = el[a + GL + e] - gl_new[e]
            el[new + GR + e] = el[b + GR + e] - gr_new[e]
            facs[i * 65 + e] = inv[e]
        for e in range(B * B):
            el[new + CC + e] = c_new[e // B][e % B]
            facs[i * 65 + NSYM + e] = w[e // B][e % B]
            facs[i * 65 + NSYM + B * B + e] = u[e // B][e % B]
        return carry

    lax.fori_loop(0, 3, merge, 0)

    diag0 = 1.0 + dv[0]
    for e in range(NMAT):
        value = el[6 * NMAT + e]
        if e < NSYM and SYM[e][0] == SYM[e][1]:
            value = value + diag0
        msend[pl.ds(e, 4, stride=MROWS), :] = value

    pl.semaphore_wait(barrier, len(peers) + 4 - solvers_here)

    halo = []

    def send_halo(src, dst, index, peer):
        copy = pltpu.make_async_remote_copy(
            src_ref=src,
            dst_ref=dst,
            send_sem=hsend.at[index],
            recv_sem=hrecv.at[index],
            device_id=peer,
            device_id_type=MESH,
        )
        copy.start()
        halo.append(copy)

    send_halo(fv.at[0, pl.ds(ncomp - B, B)], xl, 0, {"line": lax.rem(p + 1, n)})
    send_halo(fv.at[0, pl.ds(0, B)], xr, 1, {"line": lax.rem(p + n - 1, n)})
    send_halo(ysr, yl, 2, {"py": lax.rem(py + 1, npy)})
    send_halo(ysl, yr, 3, {"py": lax.rem(py + npy - 1, npy)})
    send_halo(zsr, zl, 4, {"pz": lax.rem(pz + 1, npz)})
    send_halo(zsl, zr, 5, {"pz": lax.rem(pz + npz - 1, npz)})

    def part_copies(src, dst, rows, sent, send_sem, recv_sem, s):
        here = src.at[pl.ds(s * rows, sent)]
        there = dst.at[pl.ds(pl.multiple_of(p * rows, 8), sent)]
        away = pltpu.make_async_remote_copy(
            src_ref=here,
            dst_ref=there,
            send_sem=send_sem.at[s],
            recv_sem=recv_sem.at[p],
            device_id={"line": solver[s]},
            device_id_type=MESH,
        )
        return away, pltpu.make_async_copy(here, there, send_sem.at[s])

    def start_parts(src, dst, rows, sent, send_sem, recv_sem):
        for s in range(4):
            away, near = part_copies(src, dst, rows, sent, send_sem, recv_sem, s)
            pl.when(solver[s] != p)(away.start)
            pl.when(solver[s] == p)(near.start)

    def finish_parts(src, dst, rows, sent, send_sem, recv_sem):
        for s in range(4):
            away, near = part_copies(src, dst, rows, sent, send_sem, recv_sem, s)
            pl.when(solver[s] != p)(away.wait_send)
            pl.when(solver[s] == p)(near.wait)

    def await_parts(src, dst, rows, sent, send_sem, recv_sem):
        def one(q, carry):
            copy = pltpu.make_async_remote_copy(
                src_ref=src.at[pl.ds(0, sent)],
                dst_ref=dst.at[pl.ds(pl.multiple_of(q * rows, 8), sent)],
                send_sem=send_sem.at[0],
                recv_sem=recv_sem.at[q],
                device_id={"line": solver[0]},
                device_id_type=MESH,
            )
            pl.when(q != p)(copy.wait_recv)
            return carry

        lax.fori_loop(0, n, one, 0)

    mats = (msend, mrecv, MROWS, NMAT, m_s, m_r)
    sides = (gsend, grecv, GROWS, GSEND, g_s, g_r)
    start_parts(*mats)

    for copy in halo:
        copy.wait_recv()

    x_first = jnp.where(p > 0, 0.5, 0.0)
    x_last = jnp.where(p < n - 1, -0.5, 0.0)
    y_first = jnp.where(row == 0, jnp.where(py > 0, 0.5, 0.0), 0.0)
    y_last = jnp.where(row == 3, jnp.where(py < npy - 1, -0.5, 0.0), 0.0)
    z_first = jnp.where(lane == 0, jnp.where(pz > 0, 0.5, 0.0), 0.0)
    z_last = jnp.where(lane == 127, jnp.where(pz < npz - 1, -0.5, 0.0), 0.0)
    z_left, z_right = zl[...], zr[...]
    for k in range(ncomp):
        value = rv[k] + y_first * yl[k : k + 1, :] + y_last * yr[k : k + 1, :]
        value = value + z_first * pltpu.roll(z_left, (128 - k) % 128, 1)
        value = value + z_last * pltpu.roll(z_right, 127 - k, 1)
        if k < B:
            value = value + x_first * xl[k]
        if k >= ncomp - B:
            value = value + x_last * xr[k - ncomp + B]
        rv[k] = value

    def sym_face(f):
        return [jv[f * B * B + i * B + k] for i, k in SYM]

    keep_last = jnp.where(p == n - 1, 0.0, 1.0)
    g_left, g_right = [None] * 7, [None] * 7
    for j in range(ncell // 2):
        m = 2 * j + 1
        inv = 1.0 / (1.0 + dv[m])
        scaled = [rv[m * B + i] * inv for i in range(B)]
        g_left[j] = [-v for v in sym_vec(sym_face(m - 1), scaled)]
        after = scaled if m < ncell - 1 else [v * keep_last for v in scaled]
        g_right[j] = sym_vec(sym_face(m), after)
    for i, m in enumerate((2, 6, 4)):
        a, b = 2 * i, 2 * i + 1
        q = [rv[m * B + c] + g_right[a][c] + g_left[b][c] for c in range(B)]
        w = as_mat([facs[i * 65 + NSYM + e] for e in range(B * B)])
        u = as_mat([facs[i * 65 + NSYM + B * B + e] for e in range(B * B)])
        more_l = mat_vec(transposed(w), q)
        more_r = mat_vec(transposed(u), q)
        g_left[4 + i] = [g_left[a][c] + more_l[c] for c in range(B)]
        g_right[4 + i] = [g_right[b][c] + more_r[c] for c in range(B)]
        for c in range(B):
            gel[i * B + c] = q[c]
    for c in range(B):
        gsend[pl.ds(c, 4, stride=GROWS), :] = rv[c] + g_left[6][c]
        gsend[pl.ds(B + c, 4, stride=GROWS), :] = g_right[6][c]

    start_parts(*sides)
    for i in range(3):
        value = sym_vec([facs[i * 65 + e] for e in range(NSYM)], [gel[i * B + c] for c in range(B)])
        for c in range(B):
            yv[i * B + c] = value[c]

    def answer_copy(q):
        return pltpu.make_async_remote_copy(
            src_ref=sol.at[pl.ds(pl.multiple_of(q * GROWS, 16), GSEND)],
            dst_ref=xrecv.at[pl.ds(pl.multiple_of(mine * GROWS, 16), GSEND)],
            send_sem=x_s.at[q],
            recv_sem=x_r.at[mine],
            device_id={"line": q},
            device_id_type=MESH,
        )

    own_answer = pltpu.make_async_copy(
        sol.at[pl.ds(pl.multiple_of(p * GROWS, 16), GSEND)],
        xrecv.at[pl.ds(pl.multiple_of(mine * GROWS, 16), GSEND)],
        x_s.at[p],
    )

    def solve():
        finish_parts(*mats)
        await_parts(*mats)

        def even(e):
            return mrecv[pl.ds(e, 8, stride=2 * MROWS), :]

        def odd(e):
            return mrecv[pl.ds(MROWS + e, 8, stride=2 * MROWS), :]

        inv0 = sym_inverse([odd(GL + e) + even(GR + e) for e in range(NSYM)])
        ca = as_mat([even(CC + e) for e in range(B * B)])
        cb = as_mat([odd(CC + e) for e in range(B * B)])
        w0 = sym_times(inv0, ca)
        u0 = sym_times(inv0, transposed(cb))
        less_l = product_sym(transposed(ca), w0)
        less_r = product_sym(cb, u0)
        diag = [even(GL + e) - less_l[e] + pltpu.roll(odd(GR + e) - less_r[e], 1, 0) for e in range(NSYM)]
        couple = product(cb, w0)
        base = 0

        def keep(values):
            nonlocal base
            start = base
            for value in values:
                sfac[base] = value
                base += 1
            return start

        def flat(mat):
            return [entry for line in mat for entry in line]

        at_inv0, at_w0, at_u0 = keep(inv0), keep(flat(w0)), keep(flat(u0))
        levels = []
        for step in (1, 2, 4):
            inv = sym_inverse(diag)
            left = [[pltpu.roll(entry, step, 0) for entry in line] for line in couple]
            w = sym_times(inv, left)
            u = sym_times(inv, transposed(couple))
            levels.append((step, keep(flat(w)), keep(flat(u))))
            less_l = product_sym(transposed(left), w)
            less_r = product_sym(couple, u)
            diag = [
                diag[e] - pltpu.roll(less_l[e], 8 - step, 0) - pltpu.roll(less_r[e], step, 0)
                for e in range(NSYM)
            ]
            if step < 4:
                couple = [[pltpu.roll(v, 8 - step, 0) for v in line] for line in product(couple, w)]
        at_last = keep(sym_inverse(diag))

        finish_parts(*sides)
        await_parts(*sides)

        def saved(start, count):
            return [sfac[start + e] for e in range(count)]

        def even_side(e):
            return grecv[pl.ds(e, 8, stride=2 * GROWS), :]

        def odd_side(e):
            return grecv[pl.ds(GROWS + e, 8, stride=2 * GROWS), :]

        w0 = as_mat(saved(at_w0, B * B))
        u0 = as_mat(saved(at_u0, B * B))
        q = [odd_side(c) + even_side(B + c) for c in range(B)]
        more_l = mat_vec(transposed(w0), q)
        more_r = mat_vec(transposed(u0), q)
        side = [
            even_side(c) + more_l[c] + pltpu.roll(odd_side(B + c) + more_r[c], 1, 0) for c in range(B)
        ]
        for step, at_w, at_u in levels:
            more_l = mat_vec(transposed(as_mat(saved(at_w, B * B))), side)
            more_r = mat_vec(transposed(as_mat(saved(at_u, B * B))), side)
            side = [
                side[c] + pltpu.roll(more_l[c], 8 - step, 0) + pltpu.roll(more_r[c], step, 0)
                for c in range(B)
            ]
        x_even = sym_vec(saved(at_last, NSYM), side)
        x_next = [pltpu.roll(v, 7, 0) for v in x_even]
        own = sym_vec(saved(at_inv0, NSYM), q)
        from_l = mat_vec(w0, x_even)
        from_r = mat_vec(u0, x_next)
        for c in range(B):
            x_odd = own[c] + from_l[c] + from_r[c]
            sol[pl.ds(c, 8, stride=2 * GROWS), :] = x_even[c]
            sol[pl.ds(B + c, 8, stride=2 * GROWS), :] = x_odd
            sol[pl.ds(GROWS + c, 8, stride=2 * GROWS), :] = x_odd
            sol[pl.ds(GROWS + B + c, 8, stride=2 * GROWS), :] = x_next[c]

        def send_one(q, carry):
            pl.when(q != p)(answer_copy(q).start)
            return carry

        lax.fori_loop(0, n, send_one, 0)
        own_answer.start()
        own_answer.wait()

    pl.when(is_solver)(solve)

    for s in range(4):
        copy = pltpu.make_async_remote_copy(
            src_ref=sol.at[pl.ds(0, GSEND)],
            dst_ref=xrecv.at[pl.ds(s * GROWS, GSEND)],
            send_sem=x_s.at[0],
            recv_sem=x_r.at[s],
            device_id={"line": solver[s]},
            device_id_type=MESH,
        )
        pl.when(solver[s] != p)(copy.wait_recv)

    x = [None] * (ncell + 1)
    x[0] = [xrecv[pl.ds(c, 4, stride=GROWS), :] for c in range(B)]
    x[ncell] = [xrecv[pl.ds(B + c, 4, stride=GROWS), :] for c in range(B)]
    for i, (m, a, b) in ((2, (4, 0, 8)), (0, (2, 0, 4)), (1, (6, 4, 8))):
        w = as_mat([facs[i * 65 + NSYM + e] for e in range(B * B)])
        u = as_mat([facs[i * 65 + NSYM + B * B + e] for e in range(B * B)])
        from_l, from_r = mat_vec(w, x[a]), mat_vec(u, x[b])
        x[m] = [yv[i * B + c] + from_l[c] + from_r[c] for c in range(B)]
    for m in range(1, ncell, 2):
        inv = 1.0 / (1.0 + dv[m])
        from_l = sym_vec(sym_face(m - 1), x[m - 1])
        after = x[m + 1] if m < ncell - 1 else [v * keep_last for v in x[m + 1]]
        from_r = sym_vec(sym_face(m), after)
        x[m] = [(rv[m * B + c] + from_l[c] - from_r[c]) * inv for c in range(B)]
    for m in range(ncell):
        for c in range(B):
            out_ref[m * B + c] = x[m][c]

    for copy in halo:
        copy.wait_send()

    def others():
        finish_parts(*mats)
        finish_parts(*sides)

    pl.when(jnp.logical_not(is_solver))(others)

    def answers_sent():
        def one(q, carry):
            pl.when(q != p)(answer_copy(q).wait_send)
            return carry

        lax.fori_loop(0, n, one, 0)

    pl.when(is_solver)(answers_sent)


def per_device(sizes, fluxes, jacobian, dissipation):
    n, npy, npz = sizes
    ncell = jacobian.shape[0]
    tail = jacobian.shape[3:]
    f32 = jnp.float32
    vmem, dma = pltpu.VMEM, pltpu.SemaphoreType.DMA
    tile = lambda count: vmem((count,) + tail, f32)
    flat = lambda rows: vmem((rows, 128), f32)
    ncomp = ncell * B
    out = pl.pallas_call(
        functools.partial(kernel, n, npy, npz),
        out_shape=jax.ShapeDtypeStruct((ncomp,) + tail, f32),
        in_specs=[pl.BlockSpec(memory_space=pl.ANY)] * 3,
        out_specs=pl.BlockSpec(memory_space=pltpu.VMEM),
        scratch_shapes=[
            vmem((3, ncomp) + tail, f32),
            tile(ncell * B * B),
            tile(ncell),
            tile(B),
            tile(B),
            flat(ncomp),
            flat(ncomp),
            vmem(tail, f32),
            vmem(tail, f32),
            flat(ncomp),
            flat(ncomp),
            vmem(tail, f32),
            vmem(tail, f32),
            tile(ncomp),
            tile(7 * NMAT),
            tile(3 * 65),
            tile(3 * B),
            tile(3 * B),
            flat(4 * MROWS),
            flat(n * MROWS),
            flat(4 * GROWS),
            flat(n * GROWS),
            vmem((256, 8, 128), f32),
            flat(n * GROWS),
            flat(4 * GROWS),
            dma((3,)),
            dma((6,)),
            dma((6,)),
            dma((4,)),
            dma((n,)),
            dma((4,)),
            dma((n,)),
            dma((n,)),
            dma((4,)),
        ],
        compiler_params=pltpu.CompilerParams(
            collective_id=0, has_side_effects=True, vmem_limit_bytes=60 * 1024 * 1024
        ),
    )(
        fluxes.reshape((3, ncomp) + tail),
        jacobian.reshape((ncell * B * B,) + tail),
        dissipation,
    )
    return out.reshape((ncell, B) + tail)


def solution(mesh):
    sizes = tuple(mesh.shape[name] for name in ("line", "py", "pz"))
    return jax.shard_map(
        functools.partial(per_device, sizes),
        mesh=mesh,
        in_specs=(
            P(None, "line", None, "py", "pz"),
            P("line", None, None, "py", "pz"),
            P("line", "py", "pz"),
        ),
        out_specs=P("line", None, "py", "pz"),
        check_vma=False,
    )
```

```python
import functools

import jax
import jax.numpy as jnp
from jax import lax
from jax.experimental import pallas as pl
from jax.experimental.pallas import tpu as pltpu
from jax.sharding import PartitionSpec as P

MESH = pl.DeviceIdType.MESH
B = 5
SYM = [(i, j) for i in range(B) for j in range(i, B)]
POS = {}
for _n, (_i, _j) in enumerate(SYM):
    POS[_i, _j] = POS[_j, _i] = _n
NSYM = len(SYM)
GL, GR, CC = 0, NSYM, 2 * NSYM
NMAT = 2 * NSYM + B * B
MROWS = 56
SOLVERS = ((12, 13, 14, 15), (1, 2, 3, 4))
GROWS = 16
GSEND = 2 * B


def total(terms):
    result = terms[0]
    for term in terms[1:]:
        result = result + term
    return result


def sym_inverse(a):
    a = list(a)
    for k in range(B):
        scaling = 1.0 / a[POS[k, k]]
        col = {i: a[POS[i, k]] for i in range(B) if i != k}
        scaled = {i: col[i] * scaling for i in col}
        for i, j in SYM:
            if i != k and j != k:
                a[POS[i, j]] = a[POS[i, j]] - scaled[i] * col[j]
        for i in col:
            a[POS[i, k]] = scaled[i]
        a[POS[k, k]] = -scaling
    return [-entry for entry in a]


def sym_times(inv, mat):
    return [[total([inv[POS[i, k]] * mat[k][j] for k in range(B)]) for j in range(B)] for i in range(B)]


def mat_vec(mat, vec):
    return [total([mat[i][k] * vec[k] for k in range(B)]) for i in range(B)]


def sym_vec(mat, vec):
    return [total([mat[POS[i, k]] * vec[k] for k in range(B)]) for i in range(B)]


def transposed(mat):
    return [[mat[j][i] for j in range(B)] for i in range(B)]


def product_sym(left, right):
    return [total([left[i][k] * right[k][j] for k in range(B)]) for i, j in SYM]


def product(left, right):
    return [[total([left[i][k] * right[k][j] for k in range(B)]) for j in range(B)] for i in range(B)]


def as_mat(flat):
    return [[flat[i * B + j] for j in range(B)] for i in range(B)]


def kernel(
    n,
    npy,
    npz,
    flux_hbm,
    jac_hbm,
    diss_hbm,
    out_ref,
    fv,
    jv,
    dv,
    xl,
    xr,
    yl,
    yr,
    zl,
    zr,
    ysl,
    ysr,
    zsl,
    zsr,
    rv,
    el,
    facs,
    gel,
    yv,
    msend,
    mrecv,
    gsend,
    grecv,
    sfac,
    sol,
    xrecv,
    lsem,
    hsend,
    hrecv,
    m_s,
    m_r,
    g_s,
    g_r,
    x_s,
    x_r,
):
    p = lax.axis_index("line")
    py = lax.axis_index("py")
    pz = lax.axis_index("pz")
    core = lax.rem(py, 2)
    ncell = jv.shape[0] // (B * B)
    solver = [jnp.where(core == 0, SOLVERS[0][s], SOLVERS[1][s]) for s in range(4)]
    mine = sum(jnp.where(p == solver[s], s, 0) for s in range(4))
    solvers_here = sum(jnp.where(p == solver[s], 1, 0) for s in range(4))
    is_solver = solvers_here > 0

    barrier = pltpu.get_barrier_semaphore()
    peers = [{"line": lax.rem(p + o, n)} for o in (1, n - 1)]
    peers += [{"py": lax.rem(py + o, npy)} for o in (1, npy - 1)]
    peers += [{"pz": lax.rem(pz + o, npz)} for o in (1, npz - 1)]
    def greet_line():
        for t in range(1, n):
            far = {"line": lax.rem(p + n // 2 + (t // 2 if t % 2 else n - t // 2), n)}
            pl.semaphore_signal(barrier, inc=1, device_id=far, device_id_type=MESH)

    pl.when(is_solver)(greet_line)
    for peer in peers:
        pl.semaphore_signal(barrier, inc=1, device_id=peer, device_id_type=MESH)

    loads = [
        pltpu.make_async_copy(flux_hbm, fv, lsem.at[0]),
        pltpu.make_async_copy(jac_hbm, jv, lsem.at[1]),
        pltpu.make_async_copy(diss_hbm, dv, lsem.at[2]),
    ]
    for load in loads:
        load.start()
    msend[...] = jnp.zeros_like(msend)
    gsend[...] = jnp.zeros_like(gsend)
    ncomp = ncell * B
    shape = (4, 128)
    row = lax.broadcasted_iota(jnp.int32, shape, 0)
    lane = lax.broadcasted_iota(jnp.int32, shape, 1)
    zero = jnp.zeros(shape, jnp.float32)
    loads[0].wait()

    packed_l, packed_r = zero, zero
    for k in range(ncomp):
        cell = k // B
        f_after = fv[0, k + B] if cell < ncell - 1 else zero
        f_before = fv[0, k - B] if cell > 0 else zero
        g = fv[1, k]
        h = fv[2, k]
        blank = jnp.zeros((1, 128), jnp.float32)
        dy = jnp.concatenate([g[1:], blank], 0) - jnp.concatenate([blank, g[:-1]], 0)
        h_after = jnp.where(lane == 127, 0.0, pltpu.roll(h, 127, 1))
        h_before = jnp.where(lane == 0, 0.0, pltpu.roll(h, 1, 1))
        rv[k] = -0.5 * ((f_after - f_before) + dy + (h_after - h_before))
        ysl[k : k + 1, :] = g[0:1]
        ysr[k : k + 1, :] = g[3:4]
        packed_l = jnp.where(lane == k, pltpu.roll(h, k, 1), packed_l)
        packed_r = jnp.where(lane == k, pltpu.roll(h, (k + 1) % 128, 1), packed_r)
    zsl[...] = packed_l
    zsr[...] = packed_r

    loads[1].wait()
    loads[2].wait()

    def first_level(j, carry):
        m = 2 * j + 1
        cut = jnp.logical_and(m == ncell - 1, p == n - 1)
        keep = jnp.where(cut, 0.0, 1.0)
        before = [jv[(m - 1) * B * B + i * B + k] for i, k in SYM]
        after = [jv[m * B * B + i * B + k] * keep for i, k in SYM]
        inv = 1.0 / (1.0 + dv[m])
        full_b = [[before[POS[i, k]] for k in range(B)] for i in range(B)]
        full_a = [[after[POS[i, k]] for k in range(B)] for i in range(B)]
        scaled_b = [[(before[POS[i, k]] * inv) for k in range(B)] for i in range(B)]
        scaled_a = [[(after[POS[i, k]] * inv) for k in range(B)] for i in range(B)]
        for e, value in enumerate(product_sym(full_b, scaled_b)):
            el[j * NMAT + GL + e] = value
        for e, value in enumerate(product_sym(full_a, scaled_a)):
            el[j * NMAT + GR + e] = value
        couple = product(full_a, scaled_b)
        for e in range(B * B):
            el[j * NMAT + CC + e] = couple[e // B][e % B]
        return carry

    lax.fori_loop(0, ncell // 2, first_level, 0)

    def merge(i, carry):
        a, b, new = 2 * i * NMAT, (2 * i + 1) * NMAT, (4 + i) * NMAT
        m = jnp.where(i == 2, 4, 2 + 4 * i)
        pivot = [el[a + GR + e] + el[b + GL + e] for e in range(NSYM)]
        diag = 1.0 + dv[m]
        for k in range(B):
            pivot[POS[k, k]] = pivot[POS[k, k]] + diag
        inv = sym_inverse(pivot)
        ca = as_mat([el[a + CC + e] for e in range(B * B)])
        cb = as_mat([el[b + CC + e] for e in range(B * B)])
        w = sym_times(inv, ca)
        u = sym_times(inv, transposed(cb))
        gl_new = product_sym(transposed(ca), w)
        gr_new = product_sym(cb, u)
        c_new = product(cb, w)
        for e in range(NSYM):
            el[new + GL + e] = el[a + GL + e] - gl_new[e]
            el[new + GR + e] = el[b + GR + e] - gr_new[e]
            facs[i * 65 + e] = inv[e]
        for e in range(B * B):
            el[new + CC + e] = c_new[e // B][e % B]
            facs[i * 65 + NSYM + e] = w[e // B][e % B]
            facs[i * 65 + NSYM + B * B + e] = u[e // B][e % B]
        return carry

    lax.fori_loop(0, 3, merge, 0)

    diag0 = 1.0 + dv[0]
    for e in range(NMAT):
        value = el[6 * NMAT + e]
        if e < NSYM and SYM[e][0] == SYM[e][1]:
            value = value + diag0
        msend[pl.ds(e, 4, stride=MROWS), :] = value

    pl.semaphore_wait(barrier, len(peers) + 4 - solvers_here)

    halo = []

    def send_halo(src, dst, index, peer):
        copy = pltpu.make_async_remote_copy(
            src_ref=src,
            dst_ref=dst,
            send_sem=hsend.at[index],
            recv_sem=hrecv.at[index],
            device_id=peer,
            device_id_type=MESH,
        )
        copy.start()
        halo.append(copy)

    send_halo(fv.at[0, pl.ds(ncomp - B, B)], xl, 0, {"line": lax.rem(p + 1, n)})
    send_halo(fv.at[0, pl.ds(0, B)], xr, 1, {"line": lax.rem(p + n - 1, n)})
    send_halo(ysr, yl, 2, {"py": lax.rem(py + 1, npy)})
    send_halo(ysl, yr, 3, {"py": lax.rem(py + npy - 1, npy)})
    send_halo(zsr, zl, 4, {"pz": lax.rem(pz + 1, npz)})
    send_halo(zsl, zr, 5, {"pz": lax.rem(pz + npz - 1, npz)})

    def part_copies(src, dst, rows, sent, send_sem, recv_sem, s):
        here = src.at[pl.ds(s * rows, sent)]
        there = dst.at[pl.ds(pl.multiple_of(p * rows, 8), sent)]
        away = pltpu.make_async_remote_copy(
            src_ref=here,
            dst_ref=there,
            send_sem=send_sem.at[s],
            recv_sem=recv_sem.at[p],
            device_id={"line": solver[s]},
            device_id_type=MESH,
        )
        return away, pltpu.make_async_copy(here, there, send_sem.at[s])

    def start_parts(src, dst, rows, sent, send_sem, recv_sem):
        for s in range(4):
            away, near = part_copies(src, dst, rows, sent, send_sem, recv_sem, s)
            pl.when(solver[s] != p)(away.start)
            pl.when(solver[s] == p)(near.start)

    def finish_parts(src, dst, rows, sent, send_sem, recv_sem):
        for s in range(4):
            away, near = part_copies(src, dst, rows, sent, send_sem, recv_sem, s)
            pl.when(solver[s] != p)(away.wait_send)
            pl.when(solver[s] == p)(near.wait)

    def await_parts(src, dst, rows, sent, send_sem, recv_sem):
        def one(q, carry):
            copy = pltpu.make_async_remote_copy(
                src_ref=src.at[pl.ds(0, sent)],
                dst_ref=dst.at[pl.ds(pl.multiple_of(q * rows, 8), sent)],
                send_sem=send_sem.at[0],
                recv_sem=recv_sem.at[q],
                device_id={"line": solver[0]},
                device_id_type=MESH,
            )
            pl.when(q != p)(copy.wait_recv)
            return carry

        lax.fori_loop(0, n, one, 0)

    mats = (msend, mrecv, MROWS, NMAT, m_s, m_r)
    sides = (gsend, grecv, GROWS, GSEND, g_s, g_r)
    start_parts(*mats)

    for copy in halo:
        copy.wait_recv()

    x_first = jnp.where(p > 0, 0.5, 0.0)
    x_last = jnp.where(p < n - 1, -0.5, 0.0)
    y_first = jnp.where(row == 0, jnp.where(py > 0, 0.5, 0.0), 0.0)
    y_last = jnp.where(row == 3, jnp.where(py < npy - 1, -0.5, 0.0), 0.0)
    z_first = jnp.where(lane == 0, jnp.where(pz > 0, 0.5, 0.0), 0.0)
    z_last = jnp.where(lane == 127, jnp.where(pz < npz - 1, -0.5, 0.0), 0.0)
    z_left, z_right = zl[...], zr[...]
    for k in range(ncomp):
        value = rv[k] + y_first * yl[k : k + 1, :] + y_last * yr[k : k + 1, :]
        value = value + z_first * pltpu.roll(z_left, (128 - k) % 128, 1)
        value = value + z_last * pltpu.roll(z_right, 127 - k, 1)
        if k < B:
            value = value + x_first * xl[k]
        if k >= ncomp - B:
            value = value + x_last * xr[k - ncomp + B]
        rv[k] = value

    def sym_face(f):
        return [jv[f * B * B + i * B + k] for i, k in SYM]

    keep_last = jnp.where(p == n - 1, 0.0, 1.0)
    g_left, g_right = [None] * 7, [None] * 7
    for j in range(ncell // 2):
        m = 2 * j + 1
        inv = 1.0 / (1.0 + dv[m])
        scaled = [rv[m * B + i] * inv for i in range(B)]
        g_left[j] = [-v for v in sym_vec(sym_face(m - 1), scaled)]
        after = scaled if m < ncell - 1 else [v * keep_last for v in scaled]
        g_right[j] = sym_vec(sym_face(m), after)
    for i, m in enumerate((2, 6, 4)):
        a, b = 2 * i, 2 * i + 1
        q = [rv[m * B + c] + g_right[a][c] + g_left[b][c] for c in range(B)]
        w = as_mat([facs[i * 65 + NSYM + e] for e in range(B * B)])
        u = as_mat([facs[i * 65 + NSYM + B * B + e] for e in range(B * B)])
        more_l = mat_vec(transposed(w), q)
        more_r = mat_vec(transposed(u), q)
        g_left[4 + i] = [g_left[a][c] + more_l[c] for c in range(B)]
        g_right[4 + i] = [g_right[b][c] + more_r[c] for c in range(B)]
        for c in range(B):
            gel[i * B + c] = q[c]
    for c in range(B):
        gsend[pl.ds(c, 4, stride=GROWS), :] = rv[c] + g_left[6][c]
        gsend[pl.ds(B + c, 4, stride=GROWS), :] = g_right[6][c]

    start_parts(*sides)
    for i in range(3):
        value = sym_vec([facs[i * 65 + e] for e in range(NSYM)], [gel[i * B + c] for c in range(B)])
        for c in range(B):
            yv[i * B + c] = value[c]

    def answer_copy(q):
        return pltpu.make_async_remote_copy(
            src_ref=sol.at[pl.ds(pl.multiple_of(q * GROWS, 16), GSEND)],
            dst_ref=xrecv.at[pl.ds(pl.multiple_of(mine * GROWS, 16), GSEND)],
            send_sem=x_s.at[q],
            recv_sem=x_r.at[mine],
            device_id={"line": q},
            device_id_type=MESH,
        )

    own_answer = pltpu.make_async_copy(
        sol.at[pl.ds(pl.multiple_of(p * GROWS, 16), GSEND)],
        xrecv.at[pl.ds(pl.multiple_of(mine * GROWS, 16), GSEND)],
        x_s.at[p],
    )

    def solve():
        finish_parts(*mats)
        await_parts(*mats)

        def even(e):
            return mrecv[pl.ds(e, 8, stride=2 * MROWS), :]

        def odd(e):
            return mrecv[pl.ds(MROWS + e, 8, stride=2 * MROWS), :]

        inv0 = sym_inverse([odd(GL + e) + even(GR + e) for e in range(NSYM)])
        ca = as_mat([even(CC + e) for e in range(B * B)])
        cb = as_mat([odd(CC + e) for e in range(B * B)])
        w0 = sym_times(inv0, ca)
        u0 = sym_times(inv0, transposed(cb))
        less_l = product_sym(transposed(ca), w0)
        less_r = product_sym(cb, u0)
        diag = [even(GL + e) - less_l[e] + pltpu.roll(odd(GR + e) - less_r[e], 1, 0) for e in range(NSYM)]
        couple = product(cb, w0)
        base = 0

        def keep(values):
            nonlocal base
            start = base
            for value in values:
                sfac[base] = value
                base += 1
            return start

        def flat(mat):
            return [entry for line in mat for entry in line]

        at_inv0, at_w0, at_u0 = keep(inv0), keep(flat(w0)), keep(flat(u0))
        levels = []
        for step in (1, 2, 4):
            inv = sym_inverse(diag)
            left = [[pltpu.roll(entry, step, 0) for entry in line] for line in couple]
            w = sym_times(inv, left)
            u = sym_times(inv, transposed(couple))
            levels.append((step, keep(flat(w)), keep(flat(u))))
            less_l = product_sym(transposed(left), w)
            less_r = product_sym(couple, u)
            diag = [
                diag[e] - pltpu.roll(less_l[e], 8 - step, 0) - pltpu.roll(less_r[e], step, 0)
                for e in range(NSYM)
            ]
            if step < 4:
                couple = [[pltpu.roll(v, 8 - step, 0) for v in line] for line in product(couple, w)]
        at_last = keep(sym_inverse(diag))

        finish_parts(*sides)
        await_parts(*sides)

        def saved(start, count):
            return [sfac[start + e] for e in range(count)]

        def even_side(e):
            return grecv[pl.ds(e, 8, stride=2 * GROWS), :]

        def odd_side(e):
            return grecv[pl.ds(GROWS + e, 8, stride=2 * GROWS), :]

        w0 = as_mat(saved(at_w0, B * B))
        u0 = as_mat(saved(at_u0, B * B))
        q = [odd_side(c) + even_side(B + c) for c in range(B)]
        more_l = mat_vec(transposed(w0), q)
        more_r = mat_vec(transposed(u0), q)
        side = [
            even_side(c) + more_l[c] + pltpu.roll(odd_side(B + c) + more_r[c], 1, 0) for c in range(B)
        ]
        for step, at_w, at_u in levels:
            more_l = mat_vec(transposed(as_mat(saved(at_w, B * B))), side)
            more_r = mat_vec(transposed(as_mat(saved(at_u, B * B))), side)
            side = [
                side[c] + pltpu.roll(more_l[c], 8 - step, 0) + pltpu.roll(more_r[c], step, 0)
                for c in range(B)
            ]
        x_even = sym_vec(saved(at_last, NSYM), side)
        x_next = [pltpu.roll(v, 7, 0) for v in x_even]
        own = sym_vec(saved(at_inv0, NSYM), q)
        from_l = mat_vec(w0, x_even)
        from_r = mat_vec(u0, x_next)
        for c in range(B):
            x_odd = own[c] + from_l[c] + from_r[c]
            sol[pl.ds(c, 8, stride=2 * GROWS), :] = x_even[c]
            sol[pl.ds(B + c, 8, stride=2 * GROWS), :] = x_odd
            sol[pl.ds(GROWS + c, 8, stride=2 * GROWS), :] = x_odd
            sol[pl.ds(GROWS + B + c, 8, stride=2 * GROWS), :] = x_next[c]

        def send_one(q, carry):
            pl.when(q != p)(answer_copy(q).start)
            return carry

        lax.fori_loop(0, n, send_one, 0)
        own_answer.start()
        own_answer.wait()

    pl.when(is_solver)(solve)

    for s in range(4):
        copy = pltpu.make_async_remote_copy(
            src_ref=sol.at[pl.ds(0, GSEND)],
            dst_ref=xrecv.at[pl.ds(s * GROWS, GSEND)],
            send_sem=x_s.at[0],
            recv_sem=x_r.at[s],
            device_id={"line": solver[s]},
            device_id_type=MESH,
        )
        pl.when(solver[s] != p)(copy.wait_recv)

    x = [None] * (ncell + 1)
    x[0] = [xrecv[pl.ds(c, 4, stride=GROWS), :] for c in range(B)]
    x[ncell] = [xrecv[pl.ds(B + c, 4, stride=GROWS), :] for c in range(B)]
    for i, (m, a, b) in ((2, (4, 0, 8)), (0, (2, 0, 4)), (1, (6, 4, 8))):
        w = as_mat([facs[i * 65 + NSYM + e] for e in range(B * B)])
        u = as_mat([facs[i * 65 + NSYM + B * B + e] for e in range(B * B)])
        from_l, from_r = mat_vec(w, x[a]), mat_vec(u, x[b])
        x[m] = [yv[i * B + c] + from_l[c] + from_r[c] for c in range(B)]
    for m in range(1, ncell, 2):
        inv = 1.0 / (1.0 + dv[m])
        from_l = sym_vec(sym_face(m - 1), x[m - 1])
        after = x[m + 1] if m < ncell - 1 else [v * keep_last for v in x[m + 1]]
        from_r = sym_vec(sym_face(m), after)
        x[m] = [(rv[m * B + c] + from_l[c] - from_r[c]) * inv for c in range(B)]
    for m in range(ncell):
        for c in range(B):
            out_ref[m * B + c] = x[m][c]

    for copy in halo:
        copy.wait_send()

    def others():
        finish_parts(*mats)
        finish_parts(*sides)

    pl.when(jnp.logical_not(is_solver))(others)

    def answers_sent():
        def one(q, carry):
            pl.when(q != p)(answer_copy(q).wait_send)
            return carry

        lax.fori_loop(0, n, one, 0)

    pl.when(is_solver)(answers_sent)


def per_device(sizes, fluxes, jacobian, dissipation):
    n, npy, npz = sizes
    ncell = jacobian.shape[0]
    tail = jacobian.shape[3:]
    f32 = jnp.float32
    vmem, dma = pltpu.VMEM, pltpu.SemaphoreType.DMA
    tile = lambda count: vmem((count,) + tail, f32)
    flat = lambda rows: vmem((rows, 128), f32)
    ncomp = ncell * B
    out = pl.pallas_call(
        functools.partial(kernel, n, npy, npz),
        out_shape=jax.ShapeDtypeStruct((ncomp,) + tail, f32),
        in_specs=[pl.BlockSpec(memory_space=pl.ANY)] * 3,
        out_specs=pl.BlockSpec(memory_space=pltpu.VMEM),
        scratch_shapes=[
            vmem((3, ncomp) + tail, f32),
            tile(ncell * B * B),
            tile(ncell),
            tile(B),
            tile(B),
            flat(ncomp),
            flat(ncomp),
            vmem(tail, f32),
            vmem(tail, f32),
            flat(ncomp),
            flat(ncomp),
            vmem(tail, f32),
            vmem(tail, f32),
            tile(ncomp),
            tile(7 * NMAT),
            tile(3 * 65),
            tile(3 * B),
            tile(3 * B),
            flat(4 * MROWS),
            flat(n * MROWS),
            flat(4 * GROWS),
            flat(n * GROWS),
            vmem((256, 8, 128), f32),
            flat(n * GROWS),
            flat(4 * GROWS),
            dma((3,)),
            dma((6,)),
            dma((6,)),
            dma((4,)),
            dma((n,)),
            dma((4,)),
            dma((n,)),
            dma((n,)),
            dma((4,)),
        ],
        compiler_params=pltpu.CompilerParams(
            collective_id=0, has_side_effects=True, vmem_limit_bytes=54936 * 1024
        ),
    )(
        fluxes.reshape((3, ncomp) + tail),
        jacobian.reshape((ncell * B * B,) + tail),
        dissipation,
    )
    return out.reshape((ncell, B) + tail)


def solution(mesh):
    sizes = tuple(mesh.shape[name] for name in ("line", "py", "pz"))
    return jax.shard_map(
        functools.partial(per_device, sizes),
        mesh=mesh,
        in_specs=(
            P(None, "line", None, "py", "pz"),
            P("line", None, None, "py", "pz"),
            P("line", "py", "pz"),
        ),
        out_specs=P("line", None, "py", "pz"),
        check_vma=False,
    )
```

```python
import functools

import jax
import jax.numpy as jnp
from jax import lax
from jax.experimental import pallas as pl
from jax.experimental.pallas import tpu as pltpu
from jax.sharding import PartitionSpec as P

MESH = pl.DeviceIdType.MESH
B = 5
SYM = [(i, j) for i in range(B) for j in range(i, B)]
POS = {}
for _n, (_i, _j) in enumerate(SYM):
    POS[_i, _j] = POS[_j, _i] = _n
NSYM = len(SYM)
GL, GR, CC = 0, NSYM, 2 * NSYM
NMAT = 2 * NSYM + B * B
MROWS = 56
SOLVERS = ((12, 13, 14, 15), (1, 2, 4, 6))
GROWS = 16
GSEND = 2 * B


def total(terms):
    result = terms[0]
    for term in terms[1:]:
        result = result + term
    return result


def sym_inverse(a):
    a = list(a)
    for k in range(B):
        scaling = 1.0 / a[POS[k, k]]
        col = {i: a[POS[i, k]] for i in range(B) if i != k}
        scaled = {i: col[i] * scaling for i in col}
        for i, j in SYM:
            if i != k and j != k:
                a[POS[i, j]] = a[POS[i, j]] - scaled[i] * col[j]
        for i in col:
            a[POS[i, k]] = scaled[i]
        a[POS[k, k]] = -scaling
    return [-entry for entry in a]


def sym_times(inv, mat):
    return [[total([inv[POS[i, k]] * mat[k][j] for k in range(B)]) for j in range(B)] for i in range(B)]


def mat_vec(mat, vec):
    return [total([mat[i][k] * vec[k] for k in range(B)]) for i in range(B)]


def sym_vec(mat, vec):
    return [total([mat[POS[i, k]] * vec[k] for k in range(B)]) for i in range(B)]


def transposed(mat):
    return [[mat[j][i] for j in range(B)] for i in range(B)]


def product_sym(left, right):
    return [total([left[i][k] * right[k][j] for k in range(B)]) for i, j in SYM]


def product(left, right):
    return [[total([left[i][k] * right[k][j] for k in range(B)]) for j in range(B)] for i in range(B)]


def as_mat(flat):
    return [[flat[i * B + j] for j in range(B)] for i in range(B)]


def kernel(
    n,
    npy,
    npz,
    flux_hbm,
    jac_hbm,
    diss_hbm,
    out_ref,
    fv,
    jv,
    dv,
    xl,
    xr,
    yl,
    yr,
    zl,
    zr,
    ysl,
    ysr,
    zsl,
    zsr,
    rv,
    el,
    facs,
    gel,
    yv,
    msend,
    mrecv,
    gsend,
    grecv,
    sfac,
    sol,
    xrecv,
    lsem,
    hsend,
    hrecv,
    m_s,
    m_r,
    g_s,
    g_r,
    x_s,
    x_r,
):
    p = lax.axis_index("line")
    py = lax.axis_index("py")
    pz = lax.axis_index("pz")
    core = lax.rem(py, 2)
    ncell = jv.shape[0] // (B * B)
    solver = [jnp.where(core == 0, SOLVERS[0][s], SOLVERS[1][s]) for s in range(4)]
    mine = sum(jnp.where(p == solver[s], s, 0) for s in range(4))
    solvers_here = sum(jnp.where(p == solver[s], 1, 0) for s in range(4))
    is_solver = solvers_here > 0

    barrier = pltpu.get_barrier_semaphore()
    peers = [{"line": lax.rem(p + o, n)} for o in (1, n - 1)]
    peers += [{"py": lax.rem(py + o, npy)} for o in (1, npy - 1)]
    peers += [{"pz": lax.rem(pz + o, npz)} for o in (1, npz - 1)]
    loads = [
        pltpu.make_async_copy(flux_hbm, fv, lsem.at[0]),
        pltpu.make_async_copy(jac_hbm, jv, lsem.at[1]),
        pltpu.make_async_copy(diss_hbm, dv, lsem.at[2]),
    ]
    for load in loads:
        load.start()

    def greet_line():
        for t in range(1, n):
            far = {"line": lax.rem(p + n // 2 + (t // 2 if t % 2 else n - t // 2), n)}
            pl.semaphore_signal(barrier, inc=1, device_id=far, device_id_type=MESH)

    pl.when(is_solver)(greet_line)
    for peer in peers:
        pl.semaphore_signal(barrier, inc=1, device_id=peer, device_id_type=MESH)

    msend[...] = jnp.zeros_like(msend)
    gsend[...] = jnp.zeros_like(gsend)
    ncomp = ncell * B
    shape = (4, 128)
    row = lax.broadcasted_iota(jnp.int32, shape, 0)
    lane = lax.broadcasted_iota(jnp.int32, shape, 1)
    zero = jnp.zeros(shape, jnp.float32)
    loads[0].wait()

    packed_l, packed_r = zero, zero
    for k in range(ncomp):
        cell = k // B
        f_after = fv[0, k + B] if cell < ncell - 1 else zero
        f_before = fv[0, k - B] if cell > 0 else zero
        g = fv[1, k]
        h = fv[2, k]
        blank = jnp.zeros((1, 128), jnp.float32)
        dy = jnp.concatenate([g[1:], blank], 0) - jnp.concatenate([blank, g[:-1]], 0)
        h_after = jnp.where(lane == 127, 0.0, pltpu.roll(h, 127, 1))
        h_before = jnp.where(lane == 0, 0.0, pltpu.roll(h, 1, 1))
        rv[k] = -0.5 * ((f_after - f_before) + dy + (h_after - h_before))
        ysl[k : k + 1, :] = g[0:1]
        ysr[k : k + 1, :] = g[3:4]
        packed_l = jnp.where(lane == k, pltpu.roll(h, k, 1), packed_l)
        packed_r = jnp.where(lane == k, pltpu.roll(h, (k + 1) % 128, 1), packed_r)
    zsl[...] = packed_l
    zsr[...] = packed_r

    loads[1].wait()
    loads[2].wait()

    def first_level(j, carry):
        m = 2 * j + 1
        cut = jnp.logical_and(m == ncell - 1, p == n - 1)
        keep = jnp.where(cut, 0.0, 1.0)
        before = [jv[(m - 1) * B * B + i * B + k] for i, k in SYM]
        after = [jv[m * B * B + i * B + k] * keep for i, k in SYM]
        inv = 1.0 / (1.0 + dv[m])
        full_b = [[before[POS[i, k]] for k in range(B)] for i in range(B)]
        full_a = [[after[POS[i, k]] for k in range(B)] for i in range(B)]
        scaled_b = [[(before[POS[i, k]] * inv) for k in range(B)] for i in range(B)]
        scaled_a = [[(after[POS[i, k]] * inv) for k in range(B)] for i in range(B)]
        for e, value in enumerate(product_sym(full_b, scaled_b)):
            el[j * NMAT + GL + e] = value
        for e, value in enumerate(product_sym(full_a, scaled_a)):
            el[j * NMAT + GR + e] = value
        couple = product(full_a, scaled_b)
        for e in range(B * B):
            el[j * NMAT + CC + e] = couple[e // B][e % B]
        return carry

    lax.fori_loop(0, ncell // 2, first_level, 0)

    def merge(i, carry):
        a, b, new = 2 * i * NMAT, (2 * i + 1) * NMAT, (4 + i) * NMAT
        m = jnp.where(i == 2, 4, 2 + 4 * i)
        pivot = [el[a + GR + e] + el[b + GL + e] for e in range(NSYM)]
        diag = 1.0 + dv[m]
        for k in range(B):
            pivot[POS[k, k]] = pivot[POS[k, k]] + diag
        inv = sym_inverse(pivot)
        ca = as_mat([el[a + CC + e] for e in range(B * B)])
        cb = as_mat([el[b + CC + e] for e in range(B * B)])
        w = sym_times(inv, ca)
        u = sym_times(inv, transposed(cb))
        gl_new = product_sym(transposed(ca), w)
        gr_new = product_sym(cb, u)
        c_new = product(cb, w)
        for e in range(NSYM):
            el[new + GL + e] = el[a + GL + e] - gl_new[e]
            el[new + GR + e] = el[b + GR + e] - gr_new[e]
            facs[i * 65 + e] = inv[e]
        for e in range(B * B):
            el[new + CC + e] = c_new[e // B][e % B]
            facs[i * 65 + NSYM + e] = w[e // B][e % B]
            facs[i * 65 + NSYM + B * B + e] = u[e // B][e % B]
        return carry

    lax.fori_loop(0, 3, merge, 0)

    diag0 = 1.0 + dv[0]
    for e in range(NMAT):
        value = el[6 * NMAT + e]
        if e < NSYM and SYM[e][0] == SYM[e][1]:
            value = value + diag0
        msend[pl.ds(e, 4, stride=MROWS), :] = value

    pl.semaphore_wait(barrier, len(peers) + 4 - solvers_here)

    halo = []

    def send_halo(src, dst, index, peer):
        copy = pltpu.make_async_remote_copy(
            src_ref=src,
            dst_ref=dst,
            send_sem=hsend.at[index],
            recv_sem=hrecv.at[index],
            device_id=peer,
            device_id_type=MESH,
        )
        copy.start()
        halo.append(copy)

    send_halo(fv.at[0, pl.ds(ncomp - B, B)], xl, 0, {"line": lax.rem(p + 1, n)})
    send_halo(fv.at[0, pl.ds(0, B)], xr, 1, {"line": lax.rem(p + n - 1, n)})
    send_halo(ysr, yl, 2, {"py": lax.rem(py + 1, npy)})
    send_halo(ysl, yr, 3, {"py": lax.rem(py + npy - 1, npy)})
    send_halo(zsr, zl, 4, {"pz": lax.rem(pz + 1, npz)})
    send_halo(zsl, zr, 5, {"pz": lax.rem(pz + npz - 1, npz)})

    def part_copies(src, dst, rows, sent, send_sem, recv_sem, s):
        here = src.at[pl.ds(s * rows, sent)]
        there = dst.at[pl.ds(pl.multiple_of(p * rows, 8), sent)]
        away = pltpu.make_async_remote_copy(
            src_ref=here,
            dst_ref=there,
            send_sem=send_sem.at[s],
            recv_sem=recv_sem.at[p],
            device_id={"line": solver[s]},
            device_id_type=MESH,
        )
        return away, pltpu.make_async_copy(here, there, send_sem.at[s])

    def start_parts(src, dst, rows, sent, send_sem, recv_sem):
        for s in range(4):
            away, near = part_copies(src, dst, rows, sent, send_sem, recv_sem, s)
            pl.when(solver[s] != p)(away.start)
            pl.when(solver[s] == p)(near.start)

    def finish_parts(src, dst, rows, sent, send_sem, recv_sem):
        for s in range(4):
            away, near = part_copies(src, dst, rows, sent, send_sem, recv_sem, s)
            pl.when(solver[s] != p)(away.wait_send)
            pl.when(solver[s] == p)(near.wait)

    def await_parts(src, dst, rows, sent, send_sem, recv_sem):
        def one(q, carry):
            copy = pltpu.make_async_remote_copy(
                src_ref=src.at[pl.ds(0, sent)],
                dst_ref=dst.at[pl.ds(pl.multiple_of(q * rows, 8), sent)],
                send_sem=send_sem.at[0],
                recv_sem=recv_sem.at[q],
                device_id={"line": solver[0]},
                device_id_type=MESH,
            )
            pl.when(q != p)(copy.wait_recv)
            return carry

        lax.fori_loop(0, n, one, 0)

    mats = (msend, mrecv, MROWS, NMAT, m_s, m_r)
    sides = (gsend, grecv, GROWS, GSEND, g_s, g_r)
    start_parts(*mats)

    for copy in halo:
        copy.wait_recv()

    x_first = jnp.where(p > 0, 0.5, 0.0)
    x_last = jnp.where(p < n - 1, -0.5, 0.0)
    y_first = jnp.where(row == 0, jnp.where(py > 0, 0.5, 0.0), 0.0)
    y_last = jnp.where(row == 3, jnp.where(py < npy - 1, -0.5, 0.0), 0.0)
    z_first = jnp.where(lane == 0, jnp.where(pz > 0, 0.5, 0.0), 0.0)
    z_last = jnp.where(lane == 127, jnp.where(pz < npz - 1, -0.5, 0.0), 0.0)
    z_left, z_right = zl[...], zr[...]
    for k in range(ncomp):
        value = rv[k] + y_first * yl[k : k + 1, :] + y_last * yr[k : k + 1, :]
        value = value + z_first * pltpu.roll(z_left, (128 - k) % 128, 1)
        value = value + z_last * pltpu.roll(z_right, 127 - k, 1)
        if k < B:
            value = value + x_first * xl[k]
        if k >= ncomp - B:
            value = value + x_last * xr[k - ncomp + B]
        rv[k] = value

    def sym_face(f):
        return [jv[f * B * B + i * B + k] for i, k in SYM]

    keep_last = jnp.where(p == n - 1, 0.0, 1.0)
    g_left, g_right = [None] * 7, [None] * 7
    for j in range(ncell // 2):
        m = 2 * j + 1
        inv = 1.0 / (1.0 + dv[m])
        scaled = [rv[m * B + i] * inv for i in range(B)]
        g_left[j] = [-v for v in sym_vec(sym_face(m - 1), scaled)]
        after = scaled if m < ncell - 1 else [v * keep_last for v in scaled]
        g_right[j] = sym_vec(sym_face(m), after)
    for i, m in enumerate((2, 6, 4)):
        a, b = 2 * i, 2 * i + 1
        q = [rv[m * B + c] + g_right[a][c] + g_left[b][c] for c in range(B)]
        w = as_mat([facs[i * 65 + NSYM + e] for e in range(B * B)])
        u = as_mat([facs[i * 65 + NSYM + B * B + e] for e in range(B * B)])
        more_l = mat_vec(transposed(w), q)
        more_r = mat_vec(transposed(u), q)
        g_left[4 + i] = [g_left[a][c] + more_l[c] for c in range(B)]
        g_right[4 + i] = [g_right[b][c] + more_r[c] for c in range(B)]
        for c in range(B):
            gel[i * B + c] = q[c]
    for c in range(B):
        gsend[pl.ds(c, 4, stride=GROWS), :] = rv[c] + g_left[6][c]
        gsend[pl.ds(B + c, 4, stride=GROWS), :] = g_right[6][c]

    start_parts(*sides)
    for i in range(3):
        value = sym_vec([facs[i * 65 + e] for e in range(NSYM)], [gel[i * B + c] for c in range(B)])
        for c in range(B):
            yv[i * B + c] = value[c]

    def answer_copy(q):
        return pltpu.make_async_remote_copy(
            src_ref=sol.at[pl.ds(pl.multiple_of(q * GROWS, 16), GSEND)],
            dst_ref=xrecv.at[pl.ds(pl.multiple_of(mine * GROWS, 16), GSEND)],
            send_sem=x_s.at[q],
            recv_sem=x_r.at[mine],
            device_id={"line": q},
            device_id_type=MESH,
        )

    own_answer = pltpu.make_async_copy(
        sol.at[pl.ds(pl.multiple_of(p * GROWS, 16), GSEND)],
        xrecv.at[pl.ds(pl.multiple_of(mine * GROWS, 16), GSEND)],
        x_s.at[p],
    )

    def solve():
        finish_parts(*mats)
        await_parts(*mats)

        def even(e):
            return mrecv[pl.ds(e, 8, stride=2 * MROWS), :]

        def odd(e):
            return mrecv[pl.ds(MROWS + e, 8, stride=2 * MROWS), :]

        inv0 = sym_inverse([odd(GL + e) + even(GR + e) for e in range(NSYM)])
        ca = as_mat([even(CC + e) for e in range(B * B)])
        cb = as_mat([odd(CC + e) for e in range(B * B)])
        w0 = sym_times(inv0, ca)
        u0 = sym_times(inv0, transposed(cb))
        less_l = product_sym(transposed(ca), w0)
        less_r = product_sym(cb, u0)
        diag = [even(GL + e) - less_l[e] + pltpu.roll(odd(GR + e) - less_r[e], 1, 0) for e in range(NSYM)]
        couple = product(cb, w0)
        base = 0

        def keep(values):
            nonlocal base
            start = base
            for value in values:
                sfac[base] = value
                base += 1
            return start

        def flat(mat):
            return [entry for line in mat for entry in line]

        at_inv0, at_w0, at_u0 = keep(inv0), keep(flat(w0)), keep(flat(u0))
        levels = []
        for step in (1, 2, 4):
            inv = sym_inverse(diag)
            left = [[pltpu.roll(entry, step, 0) for entry in line] for line in couple]
            w = sym_times(inv, left)
            u = sym_times(inv, transposed(couple))
            levels.append((step, keep(flat(w)), keep(flat(u))))
            less_l = product_sym(transposed(left), w)
            less_r = product_sym(couple, u)
            diag = [
                diag[e] - pltpu.roll(less_l[e], 8 - step, 0) - pltpu.roll(less_r[e], step, 0)
                for e in range(NSYM)
            ]
            if step < 4:
                couple = [[pltpu.roll(v, 8 - step, 0) for v in line] for line in product(couple, w)]
        at_last = keep(sym_inverse(diag))

        finish_parts(*sides)
        await_parts(*sides)

        def saved(start, count):
            return [sfac[start + e] for e in range(count)]

        def even_side(e):
            return grecv[pl.ds(e, 8, stride=2 * GROWS), :]

        def odd_side(e):
            return grecv[pl.ds(GROWS + e, 8, stride=2 * GROWS), :]

        w0 = as_mat(saved(at_w0, B * B))
        u0 = as_mat(saved(at_u0, B * B))
        q = [odd_side(c) + even_side(B + c) for c in range(B)]
        more_l = mat_vec(transposed(w0), q)
        more_r = mat_vec(transposed(u0), q)
        side = [
            even_side(c) + more_l[c] + pltpu.roll(odd_side(B + c) + more_r[c], 1, 0) for c in range(B)
        ]
        for step, at_w, at_u in levels:
            more_l = mat_vec(transposed(as_mat(saved(at_w, B * B))), side)
            more_r = mat_vec(transposed(as_mat(saved(at_u, B * B))), side)
            side = [
                side[c] + pltpu.roll(more_l[c], 8 - step, 0) + pltpu.roll(more_r[c], step, 0)
                for c in range(B)
            ]
        x_even = sym_vec(saved(at_last, NSYM), side)
        x_next = [pltpu.roll(v, 7, 0) for v in x_even]
        own = sym_vec(saved(at_inv0, NSYM), q)
        from_l = mat_vec(w0, x_even)
        from_r = mat_vec(u0, x_next)
        for c in range(B):
            x_odd = own[c] + from_l[c] + from_r[c]
            sol[pl.ds(c, 8, stride=2 * GROWS), :] = x_even[c]
            sol[pl.ds(B + c, 8, stride=2 * GROWS), :] = x_odd
            sol[pl.ds(GROWS + c, 8, stride=2 * GROWS), :] = x_odd
            sol[pl.ds(GROWS + B + c, 8, stride=2 * GROWS), :] = x_next[c]

        def send_one(q, carry):
            pl.when(q != p)(answer_copy(q).start)
            return carry

        lax.fori_loop(0, n, send_one, 0)
        own_answer.start()
        own_answer.wait()

    pl.when(is_solver)(solve)

    for s in range(4):
        copy = pltpu.make_async_remote_copy(
            src_ref=sol.at[pl.ds(0, GSEND)],
            dst_ref=xrecv.at[pl.ds(s * GROWS, GSEND)],
            send_sem=x_s.at[0],
            recv_sem=x_r.at[s],
            device_id={"line": solver[s]},
            device_id_type=MESH,
        )
        pl.when(solver[s] != p)(copy.wait_recv)

    x = [None] * (ncell + 1)
    x[0] = [xrecv[pl.ds(c, 4, stride=GROWS), :] for c in range(B)]
    x[ncell] = [xrecv[pl.ds(B + c, 4, stride=GROWS), :] for c in range(B)]
    for i, (m, a, b) in ((2, (4, 0, 8)), (0, (2, 0, 4)), (1, (6, 4, 8))):
        w = as_mat([facs[i * 65 + NSYM + e] for e in range(B * B)])
        u = as_mat([facs[i * 65 + NSYM + B * B + e] for e in range(B * B)])
        from_l, from_r = mat_vec(w, x[a]), mat_vec(u, x[b])
        x[m] = [yv[i * B + c] + from_l[c] + from_r[c] for c in range(B)]
    for m in range(1, ncell, 2):
        inv = 1.0 / (1.0 + dv[m])
        from_l = sym_vec(sym_face(m - 1), x[m - 1])
        after = x[m + 1] if m < ncell - 1 else [v * keep_last for v in x[m + 1]]
        from_r = sym_vec(sym_face(m), after)
        x[m] = [(rv[m * B + c] + from_l[c] - from_r[c]) * inv for c in range(B)]
    for m in range(ncell):
        for c in range(B):
            out_ref[m * B + c] = x[m][c]

    for copy in halo:
        copy.wait_send()

    def others():
        finish_parts(*mats)
        finish_parts(*sides)

    pl.when(jnp.logical_not(is_solver))(others)

    def answers_sent():
        def one(q, carry):
            pl.when(q != p)(answer_copy(q).wait_send)
            return carry

        lax.fori_loop(0, n, one, 0)

    pl.when(is_solver)(answers_sent)


def per_device(sizes, fluxes, jacobian, dissipation):
    n, npy, npz = sizes
    ncell = jacobian.shape[0]
    tail = jacobian.shape[3:]
    f32 = jnp.float32
    vmem, dma = pltpu.VMEM, pltpu.SemaphoreType.DMA
    tile = lambda count: vmem((count,) + tail, f32)
    flat = lambda rows: vmem((rows, 128), f32)
    ncomp = ncell * B
    out = pl.pallas_call(
        functools.partial(kernel, n, npy, npz),
        out_shape=jax.ShapeDtypeStruct((ncomp,) + tail, f32),
        in_specs=[pl.BlockSpec(memory_space=pl.ANY)] * 3,
        out_specs=pl.BlockSpec(memory_space=pltpu.VMEM),
        scratch_shapes=[
            vmem((3, ncomp) + tail, f32),
            tile(ncell * B * B),
            tile(ncell),
            tile(B),
            tile(B),
            flat(ncomp),
            flat(ncomp),
            vmem(tail, f32),
            vmem(tail, f32),
            flat(ncomp),
            flat(ncomp),
            vmem(tail, f32),
            vmem(tail, f32),
            tile(ncomp),
            tile(7 * NMAT),
            tile(3 * 65),
            tile(3 * B),
            tile(3 * B),
            flat(4 * MROWS),
            flat(n * MROWS),
            flat(4 * GROWS),
            flat(n * GROWS),
            vmem((256, 8, 128), f32),
            flat(n * GROWS),
            flat(4 * GROWS),
            dma((3,)),
            dma((6,)),
            dma((6,)),
            dma((4,)),
            dma((n,)),
            dma((4,)),
            dma((n,)),
            dma((n,)),
            dma((4,)),
        ],
        compiler_params=pltpu.CompilerParams(
            collective_id=0, has_side_effects=True, vmem_limit_bytes=54936 * 1024
        ),
    )(
        fluxes.reshape((3, ncomp) + tail),
        jacobian.reshape((ncell * B * B,) + tail),
        dissipation,
    )
    return out.reshape((ncell, B) + tail)


def solution(mesh):
    sizes = tuple(mesh.shape[name] for name in ("line", "py", "pz"))
    return jax.shard_map(
        functools.partial(per_device, sizes),
        mesh=mesh,
        in_specs=(
            P(None, "line", None, "py", "pz"),
            P("line", None, None, "py", "pz"),
            P("line", "py", "pz"),
        ),
        out_specs=P("line", None, "py", "pz"),
        check_vma=False,
    )
```

```python
import functools

import jax
import jax.numpy as jnp
from jax import lax
from jax.experimental import pallas as pl
from jax.experimental.pallas import tpu as pltpu
from jax.sharding import PartitionSpec as P

MESH = pl.DeviceIdType.MESH
B = 5
SYM = [(i, j) for i in range(B) for j in range(i, B)]
POS = {}
for _n, (_i, _j) in enumerate(SYM):
    POS[_i, _j] = POS[_j, _i] = _n
NSYM = len(SYM)
GL, GR, CC = 0, NSYM, 2 * NSYM
NMAT = 2 * NSYM + B * B
MROWS = 56
SOLVERS = ((12, 13, 14, 15), (1, 2, 4, 6))
GROWS = 16
GSEND = 2 * B


def total(terms):
    result = terms[0]
    for term in terms[1:]:
        result = result + term
    return result


def sym_inverse(a):
    a = list(a)
    for k in range(B):
        scaling = 1.0 / a[POS[k, k]]
        col = {i: a[POS[i, k]] for i in range(B) if i != k}
        scaled = {i: col[i] * scaling for i in col}
        for i, j in SYM:
            if i != k and j != k:
                a[POS[i, j]] = a[POS[i, j]] - scaled[i] * col[j]
        for i in col:
            a[POS[i, k]] = scaled[i]
        a[POS[k, k]] = -scaling
    return [-entry for entry in a]


def sym_times(inv, mat):
    return [[total([inv[POS[i, k]] * mat[k][j] for k in range(B)]) for j in range(B)] for i in range(B)]


def mat_vec(mat, vec):
    return [total([mat[i][k] * vec[k] for k in range(B)]) for i in range(B)]


def sym_vec(mat, vec):
    return [total([mat[POS[i, k]] * vec[k] for k in range(B)]) for i in range(B)]


def transposed(mat):
    return [[mat[j][i] for j in range(B)] for i in range(B)]


def product_sym(left, right):
    return [total([left[i][k] * right[k][j] for k in range(B)]) for i, j in SYM]


def product(left, right):
    return [[total([left[i][k] * right[k][j] for k in range(B)]) for j in range(B)] for i in range(B)]


def as_mat(flat):
    return [[flat[i * B + j] for j in range(B)] for i in range(B)]


def kernel(
    n,
    npy,
    npz,
    flux_hbm,
    jac_hbm,
    diss_hbm,
    out_ref,
    fv,
    jv,
    dv,
    xl,
    xr,
    yl,
    yr,
    zl,
    zr,
    ysl,
    ysr,
    zsl,
    zsr,
    rv,
    el,
    facs,
    gel,
    yv,
    msend,
    mrecv,
    gsend,
    grecv,
    sfac,
    sol,
    xrecv,
    lsem,
    hsend,
    hrecv,
    m_s,
    m_r,
    g_s,
    g_r,
    x_s,
    x_r,
):
    p = lax.axis_index("line")
    py = lax.axis_index("py")
    pz = lax.axis_index("pz")
    core = lax.rem(py, 2)
    ncell = jv.shape[0] // (B * B)
    solver = [jnp.where(core == 0, SOLVERS[0][s], SOLVERS[1][s]) for s in range(4)]
    mine = sum(jnp.where(p == solver[s], s, 0) for s in range(4))
    solvers_here = sum(jnp.where(p == solver[s], 1, 0) for s in range(4))
    is_solver = solvers_here > 0

    barrier = pltpu.get_barrier_semaphore()
    peers = [{"line": lax.rem(p + o, n)} for o in (1, n - 1)]
    peers += [{"py": lax.rem(py + o, npy)} for o in (1, npy - 1)]
    peers += [{"pz": lax.rem(pz + o, npz)} for o in (1, npz - 1)]
    loads = [
        pltpu.make_async_copy(flux_hbm, fv, lsem.at[0]),
        pltpu.make_async_copy(jac_hbm, jv, lsem.at[1]),
        pltpu.make_async_copy(diss_hbm, dv, lsem.at[2]),
    ]
    for load in loads:
        load.start()

    def greet_line():
        for t in range(1, n):
            far = {"line": lax.rem(p + n // 2 + (t // 2 if t % 2 else n - t // 2), n)}
            pl.semaphore_signal(barrier, inc=1, device_id=far, device_id_type=MESH)

    pl.when(is_solver)(greet_line)
    for peer in peers:
        pl.semaphore_signal(barrier, inc=1, device_id=peer, device_id_type=MESH)

    msend[...] = jnp.zeros_like(msend)
    gsend[...] = jnp.zeros_like(gsend)
    ncomp = ncell * B
    shape = (4, 128)
    row = lax.broadcasted_iota(jnp.int32, shape, 0)
    lane = lax.broadcasted_iota(jnp.int32, shape, 1)
    zero = jnp.zeros(shape, jnp.float32)
    loads[0].wait()

    packed_l, packed_r = zero, zero
    for k in range(ncomp):
        cell = k // B
        f_after = fv[0, k + B] if cell < ncell - 1 else zero
        f_before = fv[0, k - B] if cell > 0 else zero
        g = fv[1, k]
        h = fv[2, k]
        blank = jnp.zeros((1, 128), jnp.float32)
        dy = jnp.concatenate([g[1:], blank], 0) - jnp.concatenate([blank, g[:-1]], 0)
        h_after = jnp.where(lane == 127, 0.0, pltpu.roll(h, 127, 1))
        h_before = jnp.where(lane == 0, 0.0, pltpu.roll(h, 1, 1))
        rv[k] = -0.5 * ((f_after - f_before) + dy + (h_after - h_before))
        ysl[k : k + 1, :] = g[0:1]
        ysr[k : k + 1, :] = g[3:4]
        packed_l = jnp.where(lane == k, pltpu.roll(h, k, 1), packed_l)
        packed_r = jnp.where(lane == k, pltpu.roll(h, (k + 1) % 128, 1), packed_r)
    zsl[...] = packed_l
    zsr[...] = packed_r

    loads[1].wait()
    loads[2].wait()

    def first_level(j, carry):
        m = 2 * j + 1
        cut = jnp.logical_and(m == ncell - 1, p == n - 1)
        keep = jnp.where(cut, 0.0, 1.0)
        before = [jv[(m - 1) * B * B + i * B + k] for i, k in SYM]
        after = [jv[m * B * B + i * B + k] * keep for i, k in SYM]
        inv = 1.0 / (1.0 + dv[m])
        full_b = [[before[POS[i, k]] for k in range(B)] for i in range(B)]
        full_a = [[after[POS[i, k]] for k in range(B)] for i in range(B)]
        scaled_b = [[(before[POS[i, k]] * inv) for k in range(B)] for i in range(B)]
        scaled_a = [[(after[POS[i, k]] * inv) for k in range(B)] for i in range(B)]
        for e, value in enumerate(product_sym(full_b, scaled_b)):
            el[j * NMAT + GL + e] = value
        for e, value in enumerate(product_sym(full_a, scaled_a)):
            el[j * NMAT + GR + e] = value
        couple = product(full_a, scaled_b)
        for e in range(B * B):
            el[j * NMAT + CC + e] = couple[e // B][e % B]
        return carry

    lax.fori_loop(0, ncell // 2, first_level, 0)

    def merge(i, carry):
        a, b, new = 2 * i * NMAT, (2 * i + 1) * NMAT, (4 + i) * NMAT
        m = jnp.where(i == 2, 4, 2 + 4 * i)
        pivot = [el[a + GR + e] + el[b + GL + e] for e in range(NSYM)]
        diag = 1.0 + dv[m]
        for k in range(B):
            pivot[POS[k, k]] = pivot[POS[k, k]] + diag
        inv = sym_inverse(pivot)
        ca = as_mat([el[a + CC + e] for e in range(B * B)])
        cb = as_mat([el[b + CC + e] for e in range(B * B)])
        w = sym_times(inv, ca)
        u = sym_times(inv, transposed(cb))
        gl_new = product_sym(transposed(ca), w)
        gr_new = product_sym(cb, u)
        c_new = product(cb, w)
        for e in range(NSYM):
            el[new + GL + e] = el[a + GL + e] - gl_new[e]
            el[new + GR + e] = el[b + GR + e] - gr_new[e]
            facs[i * 65 + e] = inv[e]
        for e in range(B * B):
            el[new + CC + e] = c_new[e // B][e % B]
            facs[i * 65 + NSYM + e] = w[e // B][e % B]
            facs[i * 65 + NSYM + B * B + e] = u[e // B][e % B]
        return carry

    lax.fori_loop(0, 3, merge, 0)

    diag0 = 1.0 + dv[0]
    for e in range(NMAT):
        value = el[6 * NMAT + e]
        if e < NSYM and SYM[e][0] == SYM[e][1]:
            value = value + diag0
        msend[pl.ds(e, 4, stride=MROWS), :] = value

    pl.semaphore_wait(barrier, len(peers) + 4 - solvers_here)

    halo = []

    def send_halo(src, dst, index, peer):
        copy = pltpu.make_async_remote_copy(
            src_ref=src,
            dst_ref=dst,
            send_sem=hsend.at[index],
            recv_sem=hrecv.at[index],
            device_id=peer,
            device_id_type=MESH,
        )
        copy.start()
        halo.append(copy)

    send_halo(fv.at[0, pl.ds(ncomp - B, B)], xl, 0, {"line": lax.rem(p + 1, n)})
    send_halo(fv.at[0, pl.ds(0, B)], xr, 1, {"line": lax.rem(p + n - 1, n)})
    send_halo(ysr, yl, 2, {"py": lax.rem(py + 1, npy)})
    send_halo(ysl, yr, 3, {"py": lax.rem(py + npy - 1, npy)})
    send_halo(zsr, zl, 4, {"pz": lax.rem(pz + 1, npz)})
    send_halo(zsl, zr, 5, {"pz": lax.rem(pz + npz - 1, npz)})

    def part_copies(src, dst, rows, sent, send_sem, recv_sem, s):
        here = src.at[pl.ds(s * rows, sent)]
        there = dst.at[pl.ds(pl.multiple_of(p * rows, 8), sent)]
        away = pltpu.make_async_remote_copy(
            src_ref=here,
            dst_ref=there,
            send_sem=send_sem.at[s],
            recv_sem=recv_sem.at[p],
            device_id={"line": solver[s]},
            device_id_type=MESH,
        )
        return away, pltpu.make_async_copy(here, there, send_sem.at[s])

    def start_parts(src, dst, rows, sent, send_sem, recv_sem):
        for s in range(4):
            away, near = part_copies(src, dst, rows, sent, send_sem, recv_sem, s)
            pl.when(solver[s] != p)(away.start)
            pl.when(solver[s] == p)(near.start)

    def finish_home(src, dst, rows, sent, send_sem, recv_sem):
        for s in range(4):
            _, near = part_copies(src, dst, rows, sent, send_sem, recv_sem, s)
            pl.when(solver[s] == p)(near.wait)

    def finish_away(src, dst, rows, sent, send_sem, recv_sem):
        for s in range(4):
            away, _ = part_copies(src, dst, rows, sent, send_sem, recv_sem, s)
            pl.when(solver[s] != p)(away.wait_send)

    def await_parts(src, dst, rows, sent, send_sem, recv_sem):
        def one(q, carry):
            copy = pltpu.make_async_remote_copy(
                src_ref=src.at[pl.ds(0, sent)],
                dst_ref=dst.at[pl.ds(pl.multiple_of(q * rows, 8), sent)],
                send_sem=send_sem.at[0],
                recv_sem=recv_sem.at[q],
                device_id={"line": solver[0]},
                device_id_type=MESH,
            )
            pl.when(q != p)(copy.wait_recv)
            return carry

        lax.fori_loop(0, n, one, 0)

    mats = (msend, mrecv, MROWS, NMAT, m_s, m_r)
    sides = (gsend, grecv, GROWS, GSEND, g_s, g_r)
    start_parts(*mats)

    for copy in halo:
        copy.wait_recv()

    x_first = jnp.where(p > 0, 0.5, 0.0)
    x_last = jnp.where(p < n - 1, -0.5, 0.0)
    y_first = jnp.where(row == 0, jnp.where(py > 0, 0.5, 0.0), 0.0)
    y_last = jnp.where(row == 3, jnp.where(py < npy - 1, -0.5, 0.0), 0.0)
    z_first = jnp.where(lane == 0, jnp.where(pz > 0, 0.5, 0.0), 0.0)
    z_last = jnp.where(lane == 127, jnp.where(pz < npz - 1, -0.5, 0.0), 0.0)
    z_left, z_right = zl[...], zr[...]
    for k in range(ncomp):
        value = rv[k] + y_first * yl[k : k + 1, :] + y_last * yr[k : k + 1, :]
        value = value + z_first * pltpu.roll(z_left, (128 - k) % 128, 1)
        value = value + z_last * pltpu.roll(z_right, 127 - k, 1)
        if k < B:
            value = value + x_first * xl[k]
        if k >= ncomp - B:
            value = value + x_last * xr[k - ncomp + B]
        rv[k] = value

    def sym_face(f):
        return [jv[f * B * B + i * B + k] for i, k in SYM]

    keep_last = jnp.where(p == n - 1, 0.0, 1.0)
    g_left, g_right = [None] * 7, [None] * 7
    for j in range(ncell // 2):
        m = 2 * j + 1
        inv = 1.0 / (1.0 + dv[m])
        scaled = [rv[m * B + i] * inv for i in range(B)]
        g_left[j] = [-v for v in sym_vec(sym_face(m - 1), scaled)]
        after = scaled if m < ncell - 1 else [v * keep_last for v in scaled]
        g_right[j] = sym_vec(sym_face(m), after)
    for i, m in enumerate((2, 6, 4)):
        a, b = 2 * i, 2 * i + 1
        q = [rv[m * B + c] + g_right[a][c] + g_left[b][c] for c in range(B)]
        w = as_mat([facs[i * 65 + NSYM + e] for e in range(B * B)])
        u = as_mat([facs[i * 65 + NSYM + B * B + e] for e in range(B * B)])
        more_l = mat_vec(transposed(w), q)
        more_r = mat_vec(transposed(u), q)
        g_left[4 + i] = [g_left[a][c] + more_l[c] for c in range(B)]
        g_right[4 + i] = [g_right[b][c] + more_r[c] for c in range(B)]
        for c in range(B):
            gel[i * B + c] = q[c]
    for c in range(B):
        gsend[pl.ds(c, 4, stride=GROWS), :] = rv[c] + g_left[6][c]
        gsend[pl.ds(B + c, 4, stride=GROWS), :] = g_right[6][c]

    start_parts(*sides)
    for i in range(3):
        value = sym_vec([facs[i * 65 + e] for e in range(NSYM)], [gel[i * B + c] for c in range(B)])
        for c in range(B):
            yv[i * B + c] = value[c]

    def answer_copy(q):
        return pltpu.make_async_remote_copy(
            src_ref=sol.at[pl.ds(pl.multiple_of(q * GROWS, 16), GSEND)],
            dst_ref=xrecv.at[pl.ds(pl.multiple_of(mine * GROWS, 16), GSEND)],
            send_sem=x_s.at[q],
            recv_sem=x_r.at[mine],
            device_id={"line": q},
            device_id_type=MESH,
        )

    own_answer = pltpu.make_async_copy(
        sol.at[pl.ds(pl.multiple_of(p * GROWS, 16), GSEND)],
        xrecv.at[pl.ds(pl.multiple_of(mine * GROWS, 16), GSEND)],
        x_s.at[p],
    )

    def solve():
        finish_home(*mats)
        await_parts(*mats)

        def even(e):
            return mrecv[pl.ds(e, 8, stride=2 * MROWS), :]

        def odd(e):
            return mrecv[pl.ds(MROWS + e, 8, stride=2 * MROWS), :]

        inv0 = sym_inverse([odd(GL + e) + even(GR + e) for e in range(NSYM)])
        ca = as_mat([even(CC + e) for e in range(B * B)])
        cb = as_mat([odd(CC + e) for e in range(B * B)])
        w0 = sym_times(inv0, ca)
        u0 = sym_times(inv0, transposed(cb))
        less_l = product_sym(transposed(ca), w0)
        less_r = product_sym(cb, u0)
        diag = [even(GL + e) - less_l[e] + pltpu.roll(odd(GR + e) - less_r[e], 1, 0) for e in range(NSYM)]
        couple = product(cb, w0)
        base = 0

        def keep(values):
            nonlocal base
            start = base
            for value in values:
                sfac[base] = value
                base += 1
            return start

        def flat(mat):
            return [entry for line in mat for entry in line]

        at_inv0, at_w0, at_u0 = keep(inv0), keep(flat(w0)), keep(flat(u0))
        levels = []
        for step in (1, 2, 4):
            inv = sym_inverse(diag)
            left = [[pltpu.roll(entry, step, 0) for entry in line] for line in couple]
            w = sym_times(inv, left)
            u = sym_times(inv, transposed(couple))
            levels.append((step, keep(flat(w)), keep(flat(u))))
            less_l = product_sym(transposed(left), w)
            less_r = product_sym(couple, u)
            diag = [
                diag[e] - pltpu.roll(less_l[e], 8 - step, 0) - pltpu.roll(less_r[e], step, 0)
                for e in range(NSYM)
            ]
            if step < 4:
                couple = [[pltpu.roll(v, 8 - step, 0) for v in line] for line in product(couple, w)]
        at_last = keep(sym_inverse(diag))

        finish_home(*sides)
        await_parts(*sides)

        def saved(start, count):
            return [sfac[start + e] for e in range(count)]

        def even_side(e):
            return grecv[pl.ds(e, 8, stride=2 * GROWS), :]

        def odd_side(e):
            return grecv[pl.ds(GROWS + e, 8, stride=2 * GROWS), :]

        w0 = as_mat(saved(at_w0, B * B))
        u0 = as_mat(saved(at_u0, B * B))
        q = [odd_side(c) + even_side(B + c) for c in range(B)]
        more_l = mat_vec(transposed(w0), q)
        more_r = mat_vec(transposed(u0), q)
        side = [
            even_side(c) + more_l[c] + pltpu.roll(odd_side(B + c) + more_r[c], 1, 0) for c in range(B)
        ]
        for step, at_w, at_u in levels:
            more_l = mat_vec(transposed(as_mat(saved(at_w, B * B))), side)
            more_r = mat_vec(transposed(as_mat(saved(at_u, B * B))), side)
            side = [
                side[c] + pltpu.roll(more_l[c], 8 - step, 0) + pltpu.roll(more_r[c], step, 0)
                for c in range(B)
            ]
        x_even = sym_vec(saved(at_last, NSYM), side)
        x_next = [pltpu.roll(v, 7, 0) for v in x_even]
        own = sym_vec(saved(at_inv0, NSYM), q)
        from_l = mat_vec(w0, x_even)
        from_r = mat_vec(u0, x_next)
        for c in range(B):
            x_odd = own[c] + from_l[c] + from_r[c]
            sol[pl.ds(c, 8, stride=2 * GROWS), :] = x_even[c]
            sol[pl.ds(B + c, 8, stride=2 * GROWS), :] = x_odd
            sol[pl.ds(GROWS + c, 8, stride=2 * GROWS), :] = x_odd
            sol[pl.ds(GROWS + B + c, 8, stride=2 * GROWS), :] = x_next[c]

        def send_one(q, carry):
            pl.when(q != p)(answer_copy(q).start)
            return carry

        lax.fori_loop(0, n, send_one, 0)
        own_answer.start()
        own_answer.wait()

    pl.when(is_solver)(solve)

    for s in range(4):
        copy = pltpu.make_async_remote_copy(
            src_ref=sol.at[pl.ds(0, GSEND)],
            dst_ref=xrecv.at[pl.ds(s * GROWS, GSEND)],
            send_sem=x_s.at[0],
            recv_sem=x_r.at[s],
            device_id={"line": solver[s]},
            device_id_type=MESH,
        )
        pl.when(solver[s] != p)(copy.wait_recv)

    x = [None] * (ncell + 1)
    x[0] = [xrecv[pl.ds(c, 4, stride=GROWS), :] for c in range(B)]
    x[ncell] = [xrecv[pl.ds(B + c, 4, stride=GROWS), :] for c in range(B)]
    for i, (m, a, b) in ((2, (4, 0, 8)), (0, (2, 0, 4)), (1, (6, 4, 8))):
        w = as_mat([facs[i * 65 + NSYM + e] for e in range(B * B)])
        u = as_mat([facs[i * 65 + NSYM + B * B + e] for e in range(B * B)])
        from_l, from_r = mat_vec(w, x[a]), mat_vec(u, x[b])
        x[m] = [yv[i * B + c] + from_l[c] + from_r[c] for c in range(B)]
    for m in range(1, ncell, 2):
        inv = 1.0 / (1.0 + dv[m])
        from_l = sym_vec(sym_face(m - 1), x[m - 1])
        after = x[m + 1] if m < ncell - 1 else [v * keep_last for v in x[m + 1]]
        from_r = sym_vec(sym_face(m), after)
        x[m] = [(rv[m * B + c] + from_l[c] - from_r[c]) * inv for c in range(B)]
    for m in range(ncell):
        for c in range(B):
            out_ref[m * B + c] = x[m][c]

    for copy in halo:
        copy.wait_send()

    finish_away(*mats)
    finish_away(*sides)

    def answers_sent():
        def one(q, carry):
            pl.when(q != p)(answer_copy(q).wait_send)
            return carry

        lax.fori_loop(0, n, one, 0)

    pl.when(is_solver)(answers_sent)


def per_device(sizes, fluxes, jacobian, dissipation):
    n, npy, npz = sizes
    ncell = jacobian.shape[0]
    tail = jacobian.shape[3:]
    f32 = jnp.float32
    vmem, dma = pltpu.VMEM, pltpu.SemaphoreType.DMA
    tile = lambda count: vmem((count,) + tail, f32)
    flat = lambda rows: vmem((rows, 128), f32)
    ncomp = ncell * B
    out = pl.pallas_call(
        functools.partial(kernel, n, npy, npz),
        out_shape=jax.ShapeDtypeStruct((ncomp,) + tail, f32),
        in_specs=[pl.BlockSpec(memory_space=pl.ANY)] * 3,
        out_specs=pl.BlockSpec(memory_space=pltpu.VMEM),
        scratch_shapes=[
            vmem((3, ncomp) + tail, f32),
            tile(ncell * B * B),
            tile(ncell),
            tile(B),
            tile(B),
            flat(ncomp),
            flat(ncomp),
            vmem(tail, f32),
            vmem(tail, f32),
            flat(ncomp),
            flat(ncomp),
            vmem(tail, f32),
            vmem(tail, f32),
            tile(ncomp),
            tile(7 * NMAT),
            tile(3 * 65),
            tile(3 * B),
            tile(3 * B),
            flat(4 * MROWS),
            flat(n * MROWS),
            flat(4 * GROWS),
            flat(n * GROWS),
            vmem((256, 8, 128), f32),
            flat(n * GROWS),
            flat(4 * GROWS),
            dma((3,)),
            dma((6,)),
            dma((6,)),
            dma((4,)),
            dma((n,)),
            dma((4,)),
            dma((n,)),
            dma((n,)),
            dma((4,)),
        ],
        compiler_params=pltpu.CompilerParams(
            collective_id=0, has_side_effects=True, vmem_limit_bytes=54936 * 1024
        ),
    )(
        fluxes.reshape((3, ncomp) + tail),
        jacobian.reshape((ncell * B * B,) + tail),
        dissipation,
    )
    return out.reshape((ncell, B) + tail)


def solution(mesh):
    sizes = tuple(mesh.shape[name] for name in ("line", "py", "pz"))
    return jax.shard_map(
        functools.partial(per_device, sizes),
        mesh=mesh,
        in_specs=(
            P(None, "line", None, "py", "pz"),
            P("line", None, None, "py", "pz"),
            P("line", "py", "pz"),
        ),
        out_specs=P("line", None, "py", "pz"),
        check_vma=False,
    )
```
